32 devices in a mesh: ep: 8 (over z, y), dp: 4 (over x, core).
Axes of the slice: x: 2, y: 2, z: 4, core: 2. Of those that a mesh axis runs over, the one named last changes fastest.
Arguments:
- tokens: bfloat16 [512, 3584], P(('ep', 'dp')), may hold values from -6 to 6
- expert_ids: int32 [512, 8], P('ep'), may hold values from 0 to 15, all different within a row; in each aligned block of 64 rows (0 to 63, 64 to 127, ...) at most 64 rows name the same one
- gate_weights: float32 [512, 8], P('ep'), may hold values from 0.1 to 0.5
- live_counts: int32 [32], P('ep'), may hold values from 9 to 16, as said below
- w_gate: bfloat16 [16, 3584, 1024], P('ep', None, 'dp'), may hold values from -0.09375 to 0.09375
- w_up: bfloat16 [16, 3584, 1024], P('ep', None, 'dp'), may hold values from -0.09375 to 0.09375
- w_down: bfloat16 [16, 1024, 3584], P('ep', 'dp'), may hold values from -0.1875 to 0.1875
Outputs:
- moe_out: bfloat16 [512, 3584], P(('ep', 'dp'))
The draws below stay inside these ranges and needn't reach their ends.
Inputs may be any that keep to these rules, and one draw needn't show every extreme that they name: `expert_ids`: each row names 8 different experts. Among the 64 rows of one index of ep (aligned blocks) no expert is named more than 64 times, a bound that some block reaches. `live_counts`: entry i counts the live tree tokens of the i-th block of 16 rows, which are its first ones; some entry equals 16.
All inputs are finite; a program needn't handle non-finite values.
Results may differ from the reference program's by a relative error of at most 0.012.
Values may be sent and summed in bfloat16 or wider, within the bound.
A program may use at most 128 MiB of HBM per device.

```python
import math
import jax
import jax.numpy as jnp
import numpy as np
from jax import lax

D = 3584
FF = 1024
TOP = 8
TOK_DEV = 16
EXPERTS = 16
FF_DEV = 256
BLOCK = 64
CAP = 64
TOKENS = 512
COUNTS = 32
N_EP = 8
N_DP = 4


def draw_live_counts(key, part):
    first_key, second_key = jax.random.split(jax.random.fold_in(key, 17))
    counts = jax.random.randint(first_key, (COUNTS,), TOK_DEV // 2 + 1, TOK_DEV + 1)
    full_index = jax.random.randint(second_key, (), 0, COUNTS)
    return jnp.where(jnp.arange(COUNTS) == full_index, TOK_DEV, counts).astype(jnp.int32)


def levels(key, shape, shards, smallest, high):
    level, own = 1.0, jax.random.fold_in(key, 6)
    for position, blocks in shards:
        heights = jnp.exp(jax.random.uniform(jax.random.fold_in(own, position), (blocks,), jnp.float32, smallest / len(shards), high / len(shards)))
        level = level * jnp.repeat(heights, shape[position] // blocks).reshape([-1 if axis == position else 1 for axis in range(len(shape))])
    return level


def assign_block(rng, own, number, rows, number_of, top, reach, lean):
    ranking = jax.random.permutation(rng, number_of)
    crowded, common = load_shares(number_of, rows * top, reach, lean, True), load_shares(number_of, rows * top, reach, lean, False)
    places = jnp.arange(number_of)

    def named(tallies, offset_by):
        used = int((tallies > 0).sum())
        fixed = max(1, used // 4)
        moved = fixed + (places - fixed + offset_by * (used - fixed)) % max(1, number_of - fixed)
        return jnp.zeros((number_of,), jnp.int32).at[ranking[jnp.where(places < fixed, places, moved)]].set(jnp.asarray(tallies, jnp.int32))

    tallies = jnp.where(number % 4 == 0, named(crowded, number // 4), named(common, number - number // 4 - 1))
    mixed = jax.random.permutation(jax.random.fold_in(own, 3), number_of)
    source_of, taker = mixed[0:number_of // 2 * 2:2], mixed[1:number_of // 2 * 2:2]
    slack = jnp.minimum(tallies[source_of] - 1, reach - tallies[taker]) // 2
    slack = jnp.where((source_of == ranking[0]) | (taker == ranking[0]) | (tallies[taker] == 0), 0, jnp.maximum(slack, 0))
    moved = jax.random.randint(jax.random.fold_in(own, 4), (number_of // 2,), 0, 1 << 20) % (slack + 1)
    tallies = tallies.at[source_of].add(-moved).at[taker].add(moved)
    items = jnp.searchsorted(jnp.cumsum(tallies), jnp.arange(rows * top), side="right").astype(jnp.int32)
    listing = items.reshape(top, rows).T
    listing = listing[jax.random.permutation(jax.random.fold_in(own, 1), rows)]
    offset_by = jax.random.randint(jax.random.fold_in(own, 2), (rows, 1), 0, top)
    return jnp.take_along_axis(listing, (jnp.arange(top)[None, :] + offset_by) % top, axis=1)


def load_shares(amount, total, most, slope, full):
    portions = [(1 << 20) // math.isqrt(grade ** slope) + 1 for grade in range(1, amount + 1)]
    largest = most if full else min(most, max(-(-total // amount), total * portions[0] // sum(portions)))
    least = 1 if total - largest >= amount - 1 else 0
    given, rest = [largest] + [least] * (amount - 1), total - largest - least * (amount - 1)
    while rest > 0:
        free = [i for i in range(1, amount) if given[i] < largest] or [i for i in range(1, amount) if given[i] < most]
        whole, left = sum([portions[i] for i in free]), rest
        for i in free:
            addition = min(most - given[i], max(1, left * portions[i] // whole), rest)
            given[i] = given[i] + addition
            rest = rest - addition
    return np.array(given)


def gaussian(stream_key, shape, width, limit, pieces=(), kind=jnp.bfloat16):
    gain = levels(stream_key, shape, pieces, -0.22, 0.18) if pieces else 1.0
    result = jax.random.normal(stream_key, shape, jnp.float32) * width * gain
    return jnp.minimum(jnp.maximum(result, -limit), limit).astype(kind)


def setup_inputs(seed: int = 0) -> dict:
    keys = jax.random.split(jax.random.key(seed), 8)
    tokens = gaussian(keys[0], (TOKENS, D), 1.0, 6.0, ((0, 32),))
    expert_ids_keys = jax.random.split(jax.random.fold_in(keys[1], 1), TOKENS // BLOCK)
    expert_ids_turns = jax.random.permutation(jax.random.fold_in(keys[1], 3), TOKENS // BLOCK)
    expert_ids = jax.vmap(lambda own, number: assign_block(jax.random.fold_in(keys[1], 2), own, number, BLOCK, EXPERTS, TOP, CAP, 2))(expert_ids_keys, expert_ids_turns).reshape((TOKENS, TOP))
    gate_weights = jnp.clip(0.1 + 0.4 * jax.random.uniform(keys[2], (TOKENS, TOP), jnp.float32) ** levels(keys[2], (TOKENS, TOP), ((0, 8),), -0.2, 0.2), 0.1, 0.5)
    live_counts = draw_live_counts(jax.random.fold_in(keys[7], 71), 0)
    w_gate = gaussian(keys[4], (EXPERTS, D, FF), D ** -0.5, 0.09375, ((0, 8), (2, 4)))
    w_up = gaussian(keys[5], (EXPERTS, D, FF), D ** -0.5, 0.09375, ((0, 8), (2, 4)))
    w_down = gaussian(keys[6], (EXPERTS, FF, D), FF ** -0.5, 0.1875, ((0, 8), (1, 4)))
    return dict(tokens=tokens, expert_ids=expert_ids, gate_weights=gate_weights, live_counts=live_counts, w_gate=w_gate, w_up=w_up, w_down=w_down)


def slot_table(block_ids, block_counts):
    row_count = block_ids.shape[0]
    top_count = block_ids.shape[1]
    per_device = row_count // block_counts.shape[0]
    positions = jnp.arange(row_count, dtype=jnp.int32)
    owners = positions // per_device
    device_ids = jnp.arange(block_counts.shape[0], dtype=jnp.int32)
    limits = jnp.sum(jnp.where(owners[:, None] == device_ids[None, :], block_counts[None, :], 0), axis=1, dtype=jnp.int32)
    live_mask = (positions % per_device) < limits
    flat_ids = block_ids.reshape(-1).astype(jnp.int32)
    live_pairs = jnp.repeat(live_mask, top_count)
    expert_range = jnp.arange(EXPERTS, dtype=jnp.int32)
    one_hot = jnp.where((flat_ids[:, None] == expert_range[None, :]) & live_pairs[:, None], 1, 0).astype(jnp.int32)
    earlier = jnp.cumsum(one_hot, axis=0, dtype=jnp.int32) - one_hot
    slot_index = jnp.sum(earlier * one_hot, axis=1, dtype=jnp.int32)
    targets = jnp.where(live_pairs, flat_ids * CAP + slot_index, -1)
    return targets.reshape(row_count, top_count).astype(jnp.int32)


def expert_apply(row_data, gate_mat, up_mat, down_mat):
    running = jnp.zeros((row_data.shape[0], down_mat.shape[1]), jnp.float32)
    for part_idx in range(N_DP):
        col_start = part_idx * FF_DEV
        gate_part = jnp.dot(row_data, gate_mat[:, col_start:col_start + FF_DEV], preferred_element_type=jnp.float32)
        up_part = jnp.dot(row_data, up_mat[:, col_start:col_start + FF_DEV], preferred_element_type=jnp.float32)
        hidden_part = (jax.nn.silu(gate_part) * up_part).astype(jnp.bfloat16)
        expert_part = jnp.dot(hidden_part, down_mat[col_start:col_start + FF_DEV, :], preferred_element_type=jnp.float32).astype(jnp.bfloat16)
        running = running + expert_part.astype(jnp.float32)
    return running


def reference(tokens, expert_ids, gate_weights, live_counts, w_gate, w_up, w_down):
    targets = jax.vmap(slot_table)(expert_ids.reshape(N_EP, BLOCK, TOP), live_counts.reshape(N_EP, N_DP))
    slot_range = jnp.arange(EXPERTS * CAP, dtype=jnp.int32)

    def dispatch_block(operands):
        block_targets, block_tokens = operands
        selection = jnp.sum(jnp.where(block_targets[:, :, None] == slot_range[None, None, :], 1.0, 0.0).astype(jnp.float32), axis=1)
        return jnp.dot(selection.T.astype(jnp.bfloat16), block_tokens, preferred_element_type=jnp.float32).astype(jnp.bfloat16)

    buffers = lax.map(dispatch_block, (targets, tokens.reshape(N_EP, BLOCK, D)))
    per_expert = buffers.reshape(N_EP, EXPERTS, CAP, D).transpose(1, 0, 2, 3).reshape(EXPERTS, N_EP * CAP, D)

    def apply_members(members):
        return expert_apply(members[0], members[1], members[2], members[3])

    results = lax.map(apply_members, (per_expert, w_gate, w_up, w_down))
    returned = results.reshape(EXPERTS, N_EP, CAP, D).transpose(1, 0, 2, 3).reshape(N_EP, EXPERTS * CAP, D)

    def combine_block(members):
        block_targets, block_gates, block_rows = members
        picked = jnp.take(block_rows, jnp.maximum(block_targets, 0), axis=0)
        weights = jnp.where(block_targets >= 0, block_gates, 0.0).astype(jnp.float32)
        return jnp.sum(weights[:, :, None] * picked, axis=1)

    combined = lax.map(combine_block, (targets, gate_weights.reshape(N_EP, BLOCK, TOP), returned))
    return combined.reshape(TOKENS, D).astype(jnp.bfloat16)
```

```python
import jax
import jax.numpy as jnp
from jax import lax
from jax.sharding import PartitionSpec as P


def slot_table(block_ids, block_counts, experts_all, capacity):
    row_count = block_ids.shape[0]
    top_count = block_ids.shape[1]
    per_device = row_count // block_counts.shape[0]
    positions = jnp.arange(row_count, dtype=jnp.int32)
    owners = positions // per_device
    device_ids = jnp.arange(block_counts.shape[0], dtype=jnp.int32)
    limits = jnp.sum(
        jnp.where(owners[:, None] == device_ids[None, :], block_counts[None, :], 0),
        axis=1,
        dtype=jnp.int32,
    )
    live_mask = positions % per_device < limits
    flat_ids = block_ids.reshape(-1)
    live_pairs = jnp.repeat(live_mask, top_count)
    expert_range = jnp.arange(experts_all, dtype=jnp.int32)
    one_hot = jnp.where(
        (flat_ids[:, None] == expert_range[None, :]) & live_pairs[:, None], 1, 0
    ).astype(jnp.int32)
    earlier = jnp.cumsum(one_hot, axis=0, dtype=jnp.int32) - one_hot
    slot_index = jnp.sum(earlier * one_hot, axis=1, dtype=jnp.int32)
    targets = jnp.where(live_pairs, flat_ids * capacity + slot_index, -1)
    return targets.reshape(row_count, top_count)


def expert_apply(slot_rows, gate_mat, up_mat, down_mat):
    gate_part = jnp.einsum(
        "sjnd,jdf->sjnf", slot_rows, gate_mat, preferred_element_type=jnp.float32
    )
    up_part = jnp.einsum("sjnd,jdf->sjnf", slot_rows, up_mat, preferred_element_type=jnp.float32)
    hidden_part = (jax.nn.silu(gate_part) * up_part).astype(jnp.bfloat16)
    return jnp.einsum(
        "sjnf,jfd->sjnd", hidden_part, down_mat, preferred_element_type=jnp.float32
    ).astype(jnp.bfloat16)


def slot_body(tokens, expert_ids, gate_weights, live_counts, w_gate, w_up, w_down):
    ep_count = lax.axis_size("ep")
    local_experts = w_gate.shape[0]
    experts_all = local_experts * ep_count
    block_rows = expert_ids.shape[0]
    top_count = expert_ids.shape[1]
    model_width = tokens.shape[1]
    capacity = 2 * block_rows * top_count // experts_all
    block_tokens = lax.all_gather(tokens, "dp", axis=0, tiled=True)
    targets = slot_table(expert_ids, live_counts, experts_all, capacity)
    slot_range = jnp.arange(experts_all * capacity, dtype=jnp.int32)
    pick_matrix = jnp.sum(
        jnp.where(targets[:, :, None] == slot_range[None, None, :], 1.0, 0.0), axis=1
    ).astype(jnp.bfloat16)
    buffer = jnp.einsum(
        "rs,rd->sd", pick_matrix, block_tokens, preferred_element_type=jnp.float32
    ).astype(jnp.bfloat16)
    buffer = buffer.reshape(ep_count, local_experts, capacity, model_width)
    arrived_rows = lax.all_to_all(buffer, "ep", split_axis=0, concat_axis=0, tiled=True)
    result = expert_apply(arrived_rows, w_gate, w_up, w_down)
    returned = lax.all_to_all(result, "ep", split_axis=0, concat_axis=0, tiled=True)
    live_pairs = targets >= 0
    safe_targets = jnp.maximum(targets, 0)
    table = returned.reshape(experts_all * capacity, model_width)
    picked = jnp.take(table, safe_targets, axis=0).astype(jnp.float32)
    weights = jnp.where(live_pairs, gate_weights, 0.0)
    combined = jnp.sum(weights[:, :, None] * picked, axis=1)
    own_rows = lax.psum_scatter(
        combined.astype(jnp.bfloat16), "dp", scatter_dimension=0, tiled=True
    )
    return own_rows


def dense_weights(block_ids, gate_weights, block_counts, experts_all):
    rows = block_ids.shape[0]
    per_device = rows // block_counts.shape[0]
    position = jnp.arange(rows, dtype=jnp.int32)
    limits = jnp.repeat(block_counts, per_device)
    live = (position % per_device) < limits
    named = block_ids[:, :, None] == jnp.arange(experts_all, dtype=jnp.int32)[None, None, :]
    weights = jnp.where(named & live[:, None, None], gate_weights[:, :, None], 0.0)
    return jnp.sum(weights, axis=1)


def dense_body(tokens, expert_ids, gate_weights, live_counts, w_gate, w_up, w_down):
    ep_count = lax.axis_size("ep")
    local_experts = w_gate.shape[0]
    experts_all = local_experts * ep_count
    own = dense_weights(expert_ids, gate_weights, live_counts, experts_all)
    first = lax.axis_index("ep") * local_experts
    table = lax.all_gather(own, "ep", axis=0, tiled=True)
    table = lax.dynamic_slice_in_dim(table, first, local_experts, axis=1)
    everyone = lax.all_gather(tokens, ("ep", "dp"), axis=0, tiled=True)
    total = None
    for j in range(local_experts):
        gate = jnp.dot(everyone, w_gate[j], preferred_element_type=jnp.float32)
        up = jnp.dot(everyone, w_up[j], preferred_element_type=jnp.float32)
        hidden = (jax.nn.silu(gate) * up * table[:, j : j + 1]).astype(jnp.bfloat16)
        part = jnp.dot(hidden, w_down[j], preferred_element_type=jnp.float32)
        total = part if total is None else total + part
    partial = lax.psum_scatter(
        total.astype(jnp.bfloat16), "ep", scatter_dimension=0, tiled=True
    )
    return lax.psum_scatter(partial, "dp", scatter_dimension=0, tiled=True)


def body(tokens, expert_ids, gate_weights, live_counts, w_gate, w_up, w_down):
    operands = (tokens, expert_ids, gate_weights, live_counts, w_gate, w_up, w_down)
    experts_all = w_gate.shape[0] * lax.axis_size("ep")
    capacity = 2 * expert_ids.shape[0] * expert_ids.shape[1] // experts_all
    if capacity >= expert_ids.shape[0]:
        return dense_body(*operands)
    return slot_body(*operands)


def solution(mesh):
    placed = (
        P(("ep", "dp"), None),
        P("ep", None),
        P("ep", None),
        P("ep"),
        P("ep", None, "dp"),
        P("ep", None, "dp"),
        P("ep", "dp", None),
    )
    return jax.shard_map(
        body, mesh=mesh, in_specs=placed, out_specs=P(("ep", "dp"), None), check_vma=False
    )
```

```python
import jax
import jax.numpy as jnp
from jax import lax
from jax.experimental import pallas as pl
from jax.experimental.pallas import tpu as pltpu
from jax.sharding import PartitionSpec as P


def slot_table(block_ids, block_counts, experts_all, capacity):
    row_count = block_ids.shape[0]
    top_count = block_ids.shape[1]
    per_device = row_count // block_counts.shape[0]
    positions = jnp.arange(row_count, dtype=jnp.int32)
    owners = positions // per_device
    device_ids = jnp.arange(block_counts.shape[0], dtype=jnp.int32)
    limits = jnp.sum(
        jnp.where(owners[:, None] == device_ids[None, :], block_counts[None, :], 0),
        axis=1,
        dtype=jnp.int32,
    )
    live_mask = positions % per_device < limits
    flat_ids = block_ids.reshape(-1)
    live_pairs = jnp.repeat(live_mask, top_count)
    expert_range = jnp.arange(experts_all, dtype=jnp.int32)
    one_hot = jnp.where(
        (flat_ids[:, None] == expert_range[None, :]) & live_pairs[:, None], 1, 0
    ).astype(jnp.int32)
    earlier = jnp.cumsum(one_hot, axis=0, dtype=jnp.int32) - one_hot
    slot_index = jnp.sum(earlier * one_hot, axis=1, dtype=jnp.int32)
    targets = jnp.where(live_pairs, flat_ids * capacity + slot_index, -1)
    return targets.reshape(row_count, top_count)


def expert_apply(slot_rows, gate_mat, up_mat, down_mat):
    gate_part = jnp.einsum(
        "sjnd,jdf->sjnf", slot_rows, gate_mat, preferred_element_type=jnp.float32
    )
    up_part = jnp.einsum("sjnd,jdf->sjnf", slot_rows, up_mat, preferred_element_type=jnp.float32)
    hidden_part = (jax.nn.silu(gate_part) * up_part).astype(jnp.bfloat16)
    return jnp.einsum(
        "sjnf,jfd->sjnd", hidden_part, down_mat, preferred_element_type=jnp.float32
    ).astype(jnp.bfloat16)


def slot_body(tokens, expert_ids, gate_weights, live_counts, w_gate, w_up, w_down):
    ep_count = lax.axis_size("ep")
    local_experts = w_gate.shape[0]
    experts_all = local_experts * ep_count
    block_rows = expert_ids.shape[0]
    top_count = expert_ids.shape[1]
    model_width = tokens.shape[1]
    capacity = 2 * block_rows * top_count // experts_all
    block_tokens = lax.all_gather(tokens, "dp", axis=0, tiled=True)
    targets = slot_table(expert_ids, live_counts, experts_all, capacity)
    slot_range = jnp.arange(experts_all * capacity, dtype=jnp.int32)
    pick_matrix = jnp.sum(
        jnp.where(targets[:, :, None] == slot_range[None, None, :], 1.0, 0.0), axis=1
    ).astype(jnp.bfloat16)
    buffer = jnp.einsum(
        "rs,rd->sd", pick_matrix, block_tokens, preferred_element_type=jnp.float32
    ).astype(jnp.bfloat16)
    buffer = buffer.reshape(ep_count, local_experts, capacity, model_width)
    arrived_rows = lax.all_to_all(buffer, "ep", split_axis=0, concat_axis=0, tiled=True)
    result = expert_apply(arrived_rows, w_gate, w_up, w_down)
    returned = lax.all_to_all(result, "ep", split_axis=0, concat_axis=0, tiled=True)
    live_pairs = targets >= 0
    safe_targets = jnp.maximum(targets, 0)
    table = returned.reshape(experts_all * capacity, model_width)
    picked = jnp.take(table, safe_targets, axis=0).astype(jnp.float32)
    weights = jnp.where(live_pairs, gate_weights, 0.0)
    combined = jnp.sum(weights[:, :, None] * picked, axis=1)
    own_rows = lax.psum_scatter(
        combined.astype(jnp.bfloat16), "dp", scatter_dimension=0, tiled=True
    )
    return own_rows


MESH = pl.DeviceIdType.MESH
LANES = 128
CHUNKS = 4


def fused_kernel(
    tokens_ref, ids_ref, gates_ref, counts_ref, gate_hbm, up_hbm, down_hbm, out_ref,
    table, partial, from_core, from_diag, from_side, from_line,
    gate_mat, up_mat, down_mat, load_sem, gs, gr, rs, rr,
):
    depth = lax.axis_size("ep") // 2
    rows, width = tokens_ref.shape
    local_experts, _, hidden = gate_hbm.shape
    experts_all = local_experts * lax.axis_size("ep")
    ep, dp = lax.axis_index("ep"), lax.axis_index("dp")
    z, y, x, c = ep // 2, ep % 2, dp // 2, dp % 2
    full = width + LANES
    half = (width // LANES // 2) * LANES

    loads = []
    for j in range(local_experts):
        down_rows = down_mat.at[pl.ds(j * hidden, hidden)]
        loads += [(gate_hbm.at[j], gate_mat.at[j]), (up_hbm.at[j], up_mat.at[j]), (down_hbm.at[j], down_rows)]
    loads = [pltpu.make_async_copy(s, d, load_sem.at[i]) for i, (s, d) in enumerate(loads)]
    for load in loads:
        load.start()

    def place(core, py, px, pz):
        return pl.multiple_of((((core * 2 + py) * 2 + px) * depth + pz) * rows, rows)

    def device(pz, py, px, core):
        return (pz * 2 + py, px * 2 + core)

    y_peer, x_peer = device(z, 1 - y, x, c), device(z, y, 1 - x, c)
    core_peer = device(z, y, x, 1 - c)
    hops = [(z + k) % depth for k in range(depth)]
    came = [(z + depth - k) % depth for k in range(depth)]
    line = [device(hops[k], y, x, c) for k in range(1, depth)]

    mine = pl.ds(place(c, y, x, z), rows)
    table[mine, 0:width] = tokens_ref[...]
    own = pl.ds(pl.multiple_of(dp * rows, rows), rows)
    ids, gates = ids_ref[own, :], gates_ref[own, :]
    lane = lax.broadcasted_iota(jnp.int32, (rows, LANES), 1)
    live = lax.broadcasted_iota(jnp.int32, (rows, LANES), 0) < counts_ref[dp]
    expert = jnp.where(lane < experts_all, lane, lane - experts_all)
    weight = jnp.zeros((rows, LANES), jnp.float32)
    for k in range(ids.shape[1]):
        weight += jnp.where(ids[:, k : k + 1] == expert, gates[:, k : k + 1], 0.0)
    weight = jnp.where(live, weight, 0.0)
    high = weight.astype(jnp.bfloat16).astype(jnp.float32)
    split = jnp.where(lane < experts_all, high, weight - high)
    table[mine, width:full] = jnp.where(lane < 2 * experts_all, split, 0.0).astype(jnp.bfloat16)

    barrier = pltpu.get_barrier_semaphore()
    peers = line + [y_peer, x_peer, core_peer]
    for peer in peers:
        pl.semaphore_signal(barrier, inc=1, device_id=peer, device_id_type=MESH)
    pl.semaphore_wait(barrier, len(peers))

    def remote(source, target, send, recv, peer):
        return pltpu.make_async_remote_copy(
            src_ref=source, dst_ref=target, send_sem=send, recv_sem=recv,
            device_id=peer, device_id_type=MESH,
        )

    def spread(kind, k, start, lo, hi, peer):
        piece = table.at[pl.ds(start, rows), lo:hi]
        return remote(piece, piece, gs.at[kind, k], gr.at[kind, k], peer)

    sent = []

    def send(*what):
        copy = spread(*what)
        copy.start()
        sent.append(copy)

    start_own = place(c, y, x, z)
    for k in range(1, depth):
        send(0, k, start_own, 0, full, line[k - 1])
    for k in range(depth):
        here = place(c, y, x, came[k])
        if k > 0:
            spread(0, k, here, 0, full, core_peer).wait_recv()
        send(1, k, here, 0, full, y_peer)
        send(2, k, here, 0, full, x_peer)
        send(5, k, here, 0, full, core_peer)
    for k in range(depth):
        here = place(c, 1 - y, x, came[k])
        spread(1, k, here, 0, full, y_peer).wait_recv()
        send(3, k, here, 0, half, x_peer)
        send(6, k, here, 0, full, core_peer)
        here = place(c, y, 1 - x, came[k])
        spread(2, k, here, 0, full, x_peer).wait_recv()
        send(4, k, here, half, full, y_peer)
        send(7, k, here, 0, full, core_peer)
    for k in range(depth):
        here = place(c, 1 - y, 1 - x, came[k])
        spread(3, k, here, 0, half, x_peer).wait_recv()
        spread(4, k, here, half, full, y_peer).wait_recv()
        send(8, k, here, 0, full, core_peer)
    for load in loads:
        load.wait()
    sides = [(y, x), (1 - y, x), (y, 1 - x), (1 - y, 1 - x)]
    for kind, (py, px) in enumerate(sides):
        for k in range(depth):
            spread(5 + kind, k, place(1 - c, py, px, came[k]), 0, full, core_peer).wait_recv()

    block = depth * rows
    chunk = 2 * block
    first = ep * local_experts
    tile = 512 if width % 512 == 0 else LANES

    def across(i, py):
        piece = pl.ds(place(1 - c, py, 0, 0), chunk)
        landing = pl.ds(pl.multiple_of(py * chunk, chunk), chunk)
        return remote(partial.at[piece], from_core.at[landing], rs.at[0, i], rr.at[0, i], core_peer)

    def corner(side):
        lo, hi = (0, half) if side == 0 else (half, width)
        piece = partial.at[pl.ds(place(c, 1 - y, 1 - x, 0), block), lo:hi]
        peer = x_peer if side == 0 else y_peer
        return remote(piece, from_diag.at[:, lo:hi], rs.at[1, side], rr.at[1, side], peer)

    def compute(i, _):
        core = jnp.where(i < 2, 1 - c, c)
        py = jnp.where(i % 2 == 0, 1 - y, y)
        start = place(core, py, 0, 0)
        span = pl.ds(start, chunk)
        extra = table[span, width:full].astype(jnp.float32)
        lanes = lax.broadcasted_iota(jnp.int32, (chunk, LANES), 1)
        parts = []
        for j in range(local_experts):
            pick = (lanes == first + j) | (lanes == experts_all + first + j)
            share = jnp.sum(jnp.where(pick, extra, 0.0), axis=1, keepdims=True)
            gate = jnp.dot(table[span, 0:width], gate_mat[j], preferred_element_type=jnp.float32)
            up = jnp.dot(table[span, 0:width], up_mat[j], preferred_element_type=jnp.float32)
            parts.append((gate / (1.0 + jnp.exp(-gate)) * up * share).astype(jnp.bfloat16))
        both = jnp.concatenate(parts, axis=1)

        @pl.loop(0, width // tile)
        def _(n):
            columns = pl.ds(pl.multiple_of(n * tile, tile), tile)
            partial[span, columns] = jnp.dot(
                both, down_mat[:, columns], preferred_element_type=jnp.float32
            ).astype(jnp.bfloat16)

        @pl.when(i < 2)
        def _():
            across(i, py).start()

        @pl.when(i >= 2)
        def _():
            across(i - 2, py).wait_recv()

            @pl.loop(0, chunk // rows)
            def _(r):
                here = pl.ds(pl.multiple_of(start + r * rows, rows), rows)
                there = pl.ds(pl.multiple_of(py * chunk + r * rows, rows), rows)
                total = partial[here, :].astype(jnp.float32) + from_core[there, :].astype(jnp.float32)
                partial[here, :] = total.astype(jnp.bfloat16)

        @pl.when(i == 2)
        def _():
            corner(0).start()
            corner(1).start()

        return 0

    lax.fori_loop(0, CHUNKS, compute, 0)

    def side_copy(side):
        start = place(c, 1 - y, x, 0) if side == 0 else place(c, y, 1 - x, 0)
        piece = partial.at[pl.ds(start, block)]
        peer = y_peer if side == 0 else x_peer
        return remote(piece, from_side.at[side], rs.at[2, side], rr.at[2, side], peer)

    for side in range(2):
        corner(side).wait_recv()
        lo, hi = (0, half) if side == 0 else (half, width)
        start = place(c, 1 - y, x, 0) if side == 0 else place(c, y, 1 - x, 0)
        for k in range(depth):
            here = pl.ds(pl.multiple_of(start + k * rows, rows), rows)
            there = pl.ds(k * rows, rows)
            total = partial[here, lo:hi].astype(jnp.float32) + from_diag[there, lo:hi].astype(jnp.float32)
            partial[here, lo:hi] = total.astype(jnp.bfloat16)
        side_copy(side).start()
    side_copy(0).wait_recv()
    side_copy(1).wait_recv()

    def line_copy(k):
        piece = partial.at[pl.ds(place(c, y, x, hops[k]), rows)]
        return remote(piece, from_line.at[k - 1], rs.at[3, k], rr.at[3, k], line[k - 1])

    def settle(pz):
        here = pl.ds(place(c, y, x, pz), rows)
        there = pl.ds(pl.multiple_of(pz * rows, rows), rows)
        total = partial[here, :].astype(jnp.float32) + from_side[0, there, :].astype(jnp.float32)
        return total + from_side[1, there, :].astype(jnp.float32)

    for k in range(1, depth):
        partial[pl.ds(place(c, y, x, hops[k]), rows), :] = settle(hops[k]).astype(jnp.bfloat16)
        line_copy(k).start()
    total = settle(z)
    for k in range(1, depth):
        line_copy(k).wait_recv()
        total += from_line[k - 1].astype(jnp.float32)
    out_ref[...] = total.astype(out_ref.dtype)

    for copy in sent:
        copy.wait_send()
    across(0, 1 - y).wait_send()
    across(1, y).wait_send()
    for side in range(2):
        corner(side).wait_send()
        side_copy(side).wait_send()
    for k in range(1, depth):
        line_copy(k).wait_send()


def fused_body(tokens, expert_ids, gate_weights, live_counts, w_gate, w_up, w_down):
    depth = lax.axis_size("ep") // 2
    rows, width = tokens.shape
    local_experts, _, hidden = w_gate.shape
    everyone = depth * 8 * rows
    vmem, hbm = pl.BlockSpec(memory_space=pltpu.VMEM), pl.BlockSpec(memory_space=pl.ANY)
    weights = local_experts * width * hidden
    return pl.pallas_call(
        fused_kernel,
        out_shape=jax.ShapeDtypeStruct((rows, width), tokens.dtype),
        in_specs=[vmem, vmem, vmem, pl.BlockSpec(memory_space=pltpu.SMEM), hbm, hbm, hbm],
        out_specs=vmem,
        scratch_shapes=[
            pltpu.VMEM((everyone, width + LANES), jnp.bfloat16),
            pltpu.VMEM((everyone, width), jnp.bfloat16),
            pltpu.VMEM((everyone // 2, width), jnp.bfloat16),
            pltpu.VMEM((depth * rows, width), jnp.bfloat16),
            pltpu.VMEM((2, depth * rows, width), jnp.bfloat16),
            pltpu.VMEM((depth - 1, rows, width), jnp.bfloat16),
            pltpu.VMEM((local_experts, width, hidden), jnp.bfloat16),
            pltpu.VMEM((local_experts, width, hidden), jnp.bfloat16),
            pltpu.VMEM((local_experts * hidden, width), jnp.bfloat16),
            pltpu.SemaphoreType.DMA((3 * local_experts,)),
            pltpu.SemaphoreType.DMA((9, depth)),
            pltpu.SemaphoreType.DMA((9, depth)),
            pltpu.SemaphoreType.DMA((4, max(depth, 2))),
            pltpu.SemaphoreType.DMA((4, max(depth, 2))),
        ],
        compiler_params=pltpu.CompilerParams(
            collective_id=0, has_side_effects=True, vmem_limit_bytes=56 << 20
        ),
        cost_estimate=pl.CostEstimate(
            flops=6 * everyone * weights, bytes_accessed=6 * weights, transcendentals=0
        ),
    )(tokens, expert_ids, gate_weights, live_counts, w_gate, w_up, w_down)


def body(tokens, expert_ids, gate_weights, live_counts, w_gate, w_up, w_down):
    operands = (tokens, expert_ids, gate_weights, live_counts, w_gate, w_up, w_down)
    ep_count, dp_count = lax.axis_size("ep"), lax.axis_size("dp")
    experts_all = w_gate.shape[0] * ep_count
    capacity = 2 * expert_ids.shape[0] * expert_ids.shape[1] // experts_all
    if capacity >= expert_ids.shape[0] and ep_count == 8 and dp_count == 4:
        return fused_body(*operands)
    return slot_body(*operands)


def solution(mesh):
    placed = (
        P(("ep", "dp"), None),
        P("ep", None),
        P("ep", None),
        P("ep"),
        P("ep", None, "dp"),
        P("ep", None, "dp"),
        P("ep", "dp", None),
    )
    return jax.shard_map(
        body, mesh=mesh, in_specs=placed, out_specs=P(("ep", "dp"), None), check_vma=False
    )
```

```python
import jax
import jax.numpy as jnp
from jax import lax
from jax.experimental import pallas as pl
from jax.experimental.pallas import tpu as pltpu
from jax.sharding import PartitionSpec as P


def slot_table(block_ids, block_counts, experts_all, capacity):
    row_count = block_ids.shape[0]
    top_count = block_ids.shape[1]
    per_device = row_count // block_counts.shape[0]
    positions = jnp.arange(row_count, dtype=jnp.int32)
    owners = positions // per_device
    device_ids = jnp.arange(block_counts.shape[0], dtype=jnp.int32)
    limits = jnp.sum(
        jnp.where(owners[:, None] == device_ids[None, :], block_counts[None, :], 0),
        axis=1,
        dtype=jnp.int32,
    )
    live_mask = positions % per_device < limits
    flat_ids = block_ids.reshape(-1)
    live_pairs = jnp.repeat(live_mask, top_count)
    expert_range = jnp.arange(experts_all, dtype=jnp.int32)
    one_hot = jnp.where(
        (flat_ids[:, None] == expert_range[None, :]) & live_pairs[:, None], 1, 0
    ).astype(jnp.int32)
    earlier = jnp.cumsum(one_hot, axis=0, dtype=jnp.int32) - one_hot
    slot_index = jnp.sum(earlier * one_hot, axis=1, dtype=jnp.int32)
    targets = jnp.where(live_pairs, flat_ids * capacity + slot_index, -1)
    return targets.reshape(row_count, top_count)


def expert_apply(slot_rows, gate_mat, up_mat, down_mat):
    gate_part = jnp.einsum(
        "sjnd,jdf->sjnf", slot_rows, gate_mat, preferred_element_type=jnp.float32
    )
    up_part = jnp.einsum("sjnd,jdf->sjnf", slot_rows, up_mat, preferred_element_type=jnp.float32)
    hidden_part = (jax.nn.silu(gate_part) * up_part).astype(jnp.bfloat16)
    return jnp.einsum(
        "sjnf,jfd->sjnd", hidden_part, down_mat, preferred_element_type=jnp.float32
    ).astype(jnp.bfloat16)


def slot_body(tokens, expert_ids, gate_weights, live_counts, w_gate, w_up, w_down):
    ep_count = lax.axis_size("ep")
    local_experts = w_gate.shape[0]
    experts_all = local_experts * ep_count
    block_rows = expert_ids.shape[0]
    top_count = expert_ids.shape[1]
    model_width = tokens.shape[1]
    capacity = 2 * block_rows * top_count // experts_all
    block_tokens = lax.all_gather(tokens, "dp", axis=0, tiled=True)
    targets = slot_table(expert_ids, live_counts, experts_all, capacity)
    slot_range = jnp.arange(experts_all * capacity, dtype=jnp.int32)
    pick_matrix = jnp.sum(
        jnp.where(targets[:, :, None] == slot_range[None, None, :], 1.0, 0.0), axis=1
    ).astype(jnp.bfloat16)
    buffer = jnp.einsum(
        "rs,rd->sd", pick_matrix, block_tokens, preferred_element_type=jnp.float32
    ).astype(jnp.bfloat16)
    buffer = buffer.reshape(ep_count, local_experts, capacity, model_width)
    arrived_rows = lax.all_to_all(buffer, "ep", split_axis=0, concat_axis=0, tiled=True)
    result = expert_apply(arrived_rows, w_gate, w_up, w_down)
    returned = lax.all_to_all(result, "ep", split_axis=0, concat_axis=0, tiled=True)
    live_pairs = targets >= 0
    safe_targets = jnp.maximum(targets, 0)
    table = returned.reshape(experts_all * capacity, model_width)
    picked = jnp.take(table, safe_targets, axis=0).astype(jnp.float32)
    weights = jnp.where(live_pairs, gate_weights, 0.0)
    combined = jnp.sum(weights[:, :, None] * picked, axis=1)
    own_rows = lax.psum_scatter(
        combined.astype(jnp.bfloat16), "dp", scatter_dimension=0, tiled=True
    )
    return own_rows


MESH = pl.DeviceIdType.MESH
LANES = 128


def fused_kernel(
    tokens_ref, ids_ref, gates_ref, counts_ref, gate_hbm, up_hbm, down_hbm, out_ref,
    table, partial, from_core, from_diag, from_side, from_line,
    gate_mat, up_mat, down_mat, hidden_rows, load_sem, gs, gr, rs, rr,
):
    depth = lax.axis_size("ep") // 2
    rows, width = tokens_ref.shape
    local_experts, _, hidden = gate_hbm.shape
    experts_all = local_experts * lax.axis_size("ep")
    ep, dp = lax.axis_index("ep"), lax.axis_index("dp")
    z, y, x, c = ep // 2, ep % 2, dp // 2, dp % 2
    full = width + LANES
    half = (width // LANES // 2) * LANES

    loads = []
    for j in range(local_experts):
        down_rows = down_mat.at[pl.ds(j * hidden, hidden)]
        loads += [(gate_hbm.at[j], gate_mat.at[j]), (up_hbm.at[j], up_mat.at[j]), (down_hbm.at[j], down_rows)]
    loads = [pltpu.make_async_copy(s, d, load_sem.at[i]) for i, (s, d) in enumerate(loads)]
    for load in loads:
        load.start()

    def place(core, py, px, pz):
        return pl.multiple_of((((py * 2 + core) * 2 + px) * depth + pz) * rows, rows)

    def device(pz, py, px, core):
        return (pz * 2 + py, px * 2 + core)

    y_peer, x_peer = device(z, 1 - y, x, c), device(z, y, 1 - x, c)
    core_peer = device(z, y, x, 1 - c)
    hops = [(z + k) % depth for k in range(depth)]
    came = [(z + depth - k) % depth for k in range(depth)]
    line = [device(hops[k], y, x, c) for k in range(1, depth)]

    mine = pl.ds(place(c, y, x, z), rows)
    table[mine, 0:width] = tokens_ref[...]
    ids, gates = ids_ref[...], gates_ref[...]
    top, group = ids.shape
    code = lax.broadcasted_iota(jnp.int32, (LANES, group), 0)
    expert = jnp.where(code < experts_all, code, code - experts_all)
    weight = jnp.zeros((LANES, group), jnp.float32)
    for k in range(top):
        weight += jnp.where(ids[k : k + 1, :] == expert, gates[k : k + 1, :], 0.0)
    high = weight.astype(jnp.bfloat16).astype(jnp.float32)
    split = jnp.where(code < experts_all, high, weight - high)
    split = jnp.where(code < 2 * experts_all, split, 0.0).astype(jnp.bfloat16)
    row = lax.broadcasted_iota(jnp.int32, (rows, group), 0)
    column = lax.broadcasted_iota(jnp.int32, (rows, group), 1)
    live = (column == dp * rows + row) & (row < counts_ref[dp])
    table[mine, width:full] = lax.dot_general(
        jnp.where(live, 1.0, 0.0).astype(jnp.bfloat16), split,
        (((1,), (1,)), ((), ())), preferred_element_type=jnp.float32,
    ).astype(jnp.bfloat16)

    barrier = pltpu.get_barrier_semaphore()
    peers = line + [y_peer, x_peer, core_peer]
    for peer in peers:
        pl.semaphore_signal(barrier, inc=1, device_id=peer, device_id_type=MESH)
    pl.semaphore_wait(barrier, len(peers))

    def remote(source, target, send, recv, peer):
        return pltpu.make_async_remote_copy(
            src_ref=source, dst_ref=target, send_sem=send, recv_sem=recv,
            device_id=peer, device_id_type=MESH,
        )

    def spread(kind, k, start, lo, hi, peer):
        piece = table.at[pl.ds(start, rows), lo:hi]
        return remote(piece, piece, gs.at[kind, k], gr.at[kind, k], peer)

    sent = []

    def send(*what):
        copy = spread(*what)
        copy.start()
        sent.append(copy)

    start_own = place(c, y, x, z)
    for k in range(1, depth):
        send(0, k, start_own, 0, full, line[k - 1])
    for k in range(depth):
        here = place(c, y, x, came[k])
        if k > 0:
            spread(0, k, here, 0, full, core_peer).wait_recv()
        send(1, k, here, 0, full, y_peer)
        send(2, k, here, 0, full, x_peer)
        send(5, k, here, 0, full, core_peer)
    for k in range(depth):
        here = place(c, 1 - y, x, came[k])
        spread(1, k, here, 0, full, y_peer).wait_recv()
        send(3, k, here, 0, half, x_peer)
        send(6, k, here, 0, full, core_peer)
        here = place(c, y, 1 - x, came[k])
        spread(2, k, here, 0, full, x_peer).wait_recv()
        send(4, k, here, half, full, y_peer)
        send(7, k, here, 0, full, core_peer)

    def finish_gather():
        for k in range(depth):
            here = place(c, 1 - y, 1 - x, came[k])
            spread(3, k, here, 0, half, x_peer).wait_recv()
            spread(4, k, here, half, full, y_peer).wait_recv()
            send(8, k, here, 0, full, core_peer)

    def meet(kind, py, px):
        for k in range(depth):
            spread(kind, k, place(1 - c, py, px, came[k]), 0, full, core_peer).wait_recv()

    block = depth * rows
    chunk = 2 * block
    first = ep * local_experts
    tile = 512 if width % 512 == 0 else LANES
    order = list(range(1, depth)) + [0]

    def emit(copy):
        copy.start()
        sent.append(copy)

    def across(i, py):
        piece = pl.ds(place(1 - c, py, 0, 0), chunk)
        landing = pl.ds(pl.multiple_of(py * chunk, chunk), chunk)
        return remote(partial.at[piece], from_core.at[landing], rs.at[0, i], rr.at[0, i], core_peer)

    def slot(py, px, k):
        return pl.ds(place(c, py, px, hops[k]), rows)

    def spot(k):
        return pl.ds(pl.multiple_of(hops[k] * rows, rows), rows)

    def corner(side, k):
        lo, hi = (0, half) if side == 0 else (half, width)
        piece = partial.at[slot(1 - y, 1 - x, k), lo:hi]
        landing = from_diag.at[spot(k), lo:hi]
        peer = x_peer if side == 0 else y_peer
        return remote(piece, landing, rs.at[1 + side, k], rr.at[1 + side, k], peer)

    def side_copy(kind, k):
        py, px, peer, side = (y, 1 - x, x_peer, 1) if kind < 5 else (1 - y, x, y_peer, 0)
        lo, hi = (0, half) if kind in (3, 6) else (half, width)
        piece = partial.at[slot(py, px, k), lo:hi]
        landing = from_side.at[side, spot(k), lo:hi]
        return remote(piece, landing, rs.at[kind, k], rr.at[kind, k], peer)

    def add_core(py, px, k):
        here = slot(py, px, k)
        there = pl.ds(pl.multiple_of(((py * 2 + px) * depth + hops[k]) * rows, rows), rows)
        total = partial[here, :].astype(jnp.float32) + from_core[there, :].astype(jnp.float32)
        partial[here, :] = total.astype(jnp.bfloat16)

    def early():
        across(0, y).wait_recv()
        for k in order:
            add_core(y, 1 - x, k)
            emit(side_copy(3, k))
        for k in order:
            add_core(y, x, k)

    def compute(i, py, between, before_down):
        start = place(0, py, 0, 0)
        span = pl.ds(start, 2 * chunk)
        extra = table[span, width:full].astype(jnp.float32)
        lanes = lax.broadcasted_iota(jnp.int32, (2 * chunk, LANES), 1)
        for j in range(local_experts):
            pick = (lanes == first + j) | (lanes == experts_all + first + j)
            share = jnp.sum(jnp.where(pick, extra, 0.0), axis=1, keepdims=True)
            gate = jnp.dot(table[span, 0:width], gate_mat[j], preferred_element_type=jnp.float32)
            up = jnp.dot(table[span, 0:width], up_mat[j], preferred_element_type=jnp.float32)
            value = gate / (1.0 + jnp.exp(-gate)) * up * share
            hidden_rows[:, j * hidden : (j + 1) * hidden] = value.astype(jnp.bfloat16)
            if j == 0:
                between()
        before_down()
        for core in (1 - c, c):
            both = hidden_rows[pl.ds(pl.multiple_of(core * chunk, chunk), chunk), :]
            target = pl.ds(place(core, py, 0, 0), chunk)

            @pl.loop(0, width // tile)
            def _(n):
                columns = pl.ds(pl.multiple_of(n * tile, tile), tile)
                partial[target, columns] = jnp.dot(
                    both, down_mat[:, columns], preferred_element_type=jnp.float32
                ).astype(jnp.bfloat16)

            if core is not c:
                emit(across(i, py))

    def nothing():
        pass

    for load in loads:
        load.wait()
    meet(5, y, x)
    meet(7, y, 1 - x)
    compute(0, y, nothing, finish_gather)
    meet(6, 1 - y, x)
    meet(8, 1 - y, 1 - x)
    compute(1, 1 - y, early, nothing)

    across(1, 1 - y).wait_recv()
    for k in order:
        add_core(1 - y, 1 - x, k)
        emit(corner(0, k))
        emit(corner(1, k))
    for k in order:
        add_core(1 - y, x, k)
        emit(side_copy(5, k))

    for k in order:
        for side, kind, py, px in ((0, 6, 1 - y, x), (1, 4, y, 1 - x)):
            corner(side, k).wait_recv()
            lo, hi = (0, half) if side == 0 else (half, width)
            here, there = slot(py, px, k), spot(k)
            total = partial[here, lo:hi].astype(jnp.float32) + from_diag[there, lo:hi].astype(jnp.float32)
            partial[here, lo:hi] = total.astype(jnp.bfloat16)
            emit(side_copy(kind, k))

    def line_copy(k):
        piece = partial.at[slot(y, x, k)]
        return remote(piece, from_line.at[k - 1], rs.at[7, k], rr.at[7, k], line[k - 1])

    def settle(k):
        for kind in (3, 4, 5, 6):
            side_copy(kind, k).wait_recv()
        there = spot(k)
        total = partial[slot(y, x, k), :].astype(jnp.float32) + from_side[0, there, :].astype(jnp.float32)
        return total + from_side[1, there, :].astype(jnp.float32)

    for k in range(1, depth):
        partial[slot(y, x, k), :] = settle(k).astype(jnp.bfloat16)
        emit(line_copy(k))
    total = settle(0)
    for k in range(1, depth):
        line_copy(k).wait_recv()
        total += from_line[k - 1].astype(jnp.float32)
    out_ref[...] = total.astype(out_ref.dtype)

    for copy in sent:
        copy.wait_send()


def fused_body(tokens, expert_ids, gate_weights, live_counts, w_gate, w_up, w_down):
    depth = lax.axis_size("ep") // 2
    rows, width = tokens.shape
    local_experts, _, hidden = w_gate.shape
    everyone = depth * 8 * rows
    vmem, hbm = pl.BlockSpec(memory_space=pltpu.VMEM), pl.BlockSpec(memory_space=pl.ANY)
    weights = local_experts * width * hidden
    return pl.pallas_call(
        fused_kernel,
        out_shape=jax.ShapeDtypeStruct((rows, width), tokens.dtype),
        in_specs=[vmem, vmem, vmem, pl.BlockSpec(memory_space=pltpu.SMEM), hbm, hbm, hbm],
        out_specs=vmem,
        scratch_shapes=[
            pltpu.VMEM((everyone, width + LANES), jnp.bfloat16),
            pltpu.VMEM((everyone, width), jnp.bfloat16),
            pltpu.VMEM((everyone // 2, width), jnp.bfloat16),
            pltpu.VMEM((depth * rows, width), jnp.bfloat16),
            pltpu.VMEM((2, depth * rows, width), jnp.bfloat16),
            pltpu.VMEM((depth - 1, rows, width), jnp.bfloat16),
            pltpu.VMEM((local_experts, width, hidden), jnp.bfloat16),
            pltpu.VMEM((local_experts, width, hidden), jnp.bfloat16),
            pltpu.VMEM((local_experts * hidden, width), jnp.bfloat16),
            pltpu.VMEM((everyone // 2, local_experts * hidden), jnp.bfloat16),
            pltpu.SemaphoreType.DMA((3 * local_experts,)),
            pltpu.SemaphoreType.DMA((9, depth)),
            pltpu.SemaphoreType.DMA((9, depth)),
            pltpu.SemaphoreType.DMA((8, max(depth, 2))),
            pltpu.SemaphoreType.DMA((8, max(depth, 2))),
        ],
        compiler_params=pltpu.CompilerParams(
            collective_id=0, has_side_effects=True, vmem_limit_bytes=56 << 20
        ),
        cost_estimate=pl.CostEstimate(
            flops=6 * everyone * weights, bytes_accessed=6 * weights, transcendentals=0
        ),
    )(tokens, expert_ids.T, gate_weights.T, live_counts, w_gate, w_up, w_down)


def body(tokens, expert_ids, gate_weights, live_counts, w_gate, w_up, w_down):
    operands = (tokens, expert_ids, gate_weights, live_counts, w_gate, w_up, w_down)
    ep_count, dp_count = lax.axis_size("ep"), lax.axis_size("dp")
    experts_all = w_gate.shape[0] * ep_count
    capacity = 2 * expert_ids.shape[0] * expert_ids.shape[1] // experts_all
    if capacity >= expert_ids.shape[0] and ep_count == 8 and dp_count == 4:
        return fused_body(*operands)
    return slot_body(*operands)


def solution(mesh):
    placed = (
        P(("ep", "dp"), None),
        P("ep", None),
        P("ep", None),
        P("ep"),
        P("ep", None, "dp"),
        P("ep", None, "dp"),
        P("ep", "dp", None),
    )
    return jax.shard_map(
        body, mesh=mesh, in_specs=placed, out_specs=P(("ep", "dp"), None), check_vma=False
    )
```

```python
import jax
import jax.numpy as jnp
from jax import lax
from jax.experimental import pallas as pl
from jax.experimental.pallas import tpu as pltpu
from jax.sharding import PartitionSpec as P


def slot_table(block_ids, block_counts, experts_all, capacity):
    row_count = block_ids.shape[0]
    top_count = block_ids.shape[1]
    per_device = row_count // block_counts.shape[0]
    positions = jnp.arange(row_count, dtype=jnp.int32)
    owners = positions // per_device
    device_ids = jnp.arange(block_counts.shape[0], dtype=jnp.int32)
    limits = jnp.sum(
        jnp.where(owners[:, None] == device_ids[None, :], block_counts[None, :], 0),
        axis=1,
        dtype=jnp.int32,
    )
    live_mask = positions % per_device < limits
    flat_ids = block_ids.reshape(-1)
    live_pairs = jnp.repeat(live_mask, top_count)
    expert_range = jnp.arange(experts_all, dtype=jnp.int32)
    one_hot = jnp.where(
        (flat_ids[:, None] == expert_range[None, :]) & live_pairs[:, None], 1, 0
    ).astype(jnp.int32)
    earlier = jnp.cumsum(one_hot, axis=0, dtype=jnp.int32) - one_hot
    slot_index = jnp.sum(earlier * one_hot, axis=1, dtype=jnp.int32)
    targets = jnp.where(live_pairs, flat_ids * capacity + slot_index, -1)
    return targets.reshape(row_count, top_count)


def expert_apply(slot_rows, gate_mat, up_mat, down_mat):
    gate_part = jnp.einsum(
        "sjnd,jdf->sjnf", slot_rows, gate_mat, preferred_element_type=jnp.float32
    )
    up_part = jnp.einsum("sjnd,jdf->sjnf", slot_rows, up_mat, preferred_element_type=jnp.float32)
    hidden_part = (jax.nn.silu(gate_part) * up_part).astype(jnp.bfloat16)
    return jnp.einsum(
        "sjnf,jfd->sjnd", hidden_part, down_mat, preferred_element_type=jnp.float32
    ).astype(jnp.bfloat16)


def slot_body(tokens, expert_ids, gate_weights, live_counts, w_gate, w_up, w_down):
    ep_count = lax.axis_size("ep")
    local_experts = w_gate.shape[0]
    experts_all = local_experts * ep_count
    block_rows = expert_ids.shape[0]
    top_count = expert_ids.shape[1]
    model_width = tokens.shape[1]
    capacity = 2 * block_rows * top_count // experts_all
    block_tokens = lax.all_gather(tokens, "dp", axis=0, tiled=True)
    targets = slot_table(expert_ids, live_counts, experts_all, capacity)
    slot_range = jnp.arange(experts_all * capacity, dtype=jnp.int32)
    pick_matrix = jnp.sum(
        jnp.where(targets[:, :, None] == slot_range[None, None, :], 1.0, 0.0), axis=1
    ).astype(jnp.bfloat16)
    buffer = jnp.einsum(
        "rs,rd->sd", pick_matrix, block_tokens, preferred_element_type=jnp.float32
    ).astype(jnp.bfloat16)
    buffer = buffer.reshape(ep_count, local_experts, capacity, model_width)
    arrived_rows = lax.all_to_all(buffer, "ep", split_axis=0, concat_axis=0, tiled=True)
    result = expert_apply(arrived_rows, w_gate, w_up, w_down)
    returned = lax.all_to_all(result, "ep", split_axis=0, concat_axis=0, tiled=True)
    live_pairs = targets >= 0
    safe_targets = jnp.maximum(targets, 0)
    table = returned.reshape(experts_all * capacity, model_width)
    picked = jnp.take(table, safe_targets, axis=0).astype(jnp.float32)
    weights = jnp.where(live_pairs, gate_weights, 0.0)
    combined = jnp.sum(weights[:, :, None] * picked, axis=1)
    own_rows = lax.psum_scatter(
        combined.astype(jnp.bfloat16), "dp", scatter_dimension=0, tiled=True
    )
    return own_rows


MESH = pl.DeviceIdType.MESH
LANES = 128


def fused_kernel(
    tokens_ref, ids_ref, gates_ref, counts_ref, gate_hbm, up_hbm, down_hbm, out_ref,
    table, partial, from_core, from_diag, from_side, from_line,
    gate_mat, up_mat, down_mat, hidden_rows, load_sem, gs, gr, rs, rr,
):
    depth = lax.axis_size("ep") // 2
    rows, width = tokens_ref.shape
    local_experts, _, hidden = gate_hbm.shape
    experts_all = local_experts * lax.axis_size("ep")
    ep, dp = lax.axis_index("ep"), lax.axis_index("dp")
    z, y, x, c = ep // 2, ep % 2, dp // 2, dp % 2
    full = width + LANES
    half = (width // LANES // 2) * LANES

    loads = []
    for j in range(local_experts):
        down_rows = down_mat.at[pl.ds(j * hidden, hidden)]
        loads += [(gate_hbm.at[j], gate_mat.at[j]), (up_hbm.at[j], up_mat.at[j]), (down_hbm.at[j], down_rows)]
    loads = [pltpu.make_async_copy(s, d, load_sem.at[i]) for i, (s, d) in enumerate(loads)]
    for load in loads:
        load.start()

    def place(core, py, px, pz):
        return pl.multiple_of((((py * 2 + core) * 2 + px) * depth + pz) * rows, rows)

    def device(pz, py, px, core):
        return (pz * 2 + py, px * 2 + core)

    y_peer, x_peer = device(z, 1 - y, x, c), device(z, y, 1 - x, c)
    core_peer = device(z, y, x, 1 - c)
    hops = [(z + k) % depth for k in range(depth)]
    nearest = [sorted(range(depth), key=lambda o, v=v: (abs(o - v), o)) for v in range(depth)]
    came = [sum(jnp.where(z == v, nearest[v][k], 0) for v in range(depth)) for k in range(depth)]
    above, below = device(z + 1, y, x, c), device(z - 1, y, x, c)
    line = [device(hops[k], y, x, c) for k in range(1, depth)]

    mine = pl.ds(place(c, y, x, z), rows)
    table[mine, 0:width] = tokens_ref[...]
    ids, gates = ids_ref[...], gates_ref[...]
    top, group = ids.shape
    code = lax.broadcasted_iota(jnp.int32, (LANES, group), 0)
    expert = jnp.where(code < experts_all, code, code - experts_all)
    weight = jnp.zeros((LANES, group), jnp.float32)
    for k in range(top):
        weight += jnp.where(ids[k : k + 1, :] == expert, gates[k : k + 1, :], 0.0)
    high = weight.astype(jnp.bfloat16).astype(jnp.float32)
    split = jnp.where(code < experts_all, high, weight - high)
    split = jnp.where(code < 2 * experts_all, split, 0.0).astype(jnp.bfloat16)
    row = lax.broadcasted_iota(jnp.int32, (rows, group), 0)
    column = lax.broadcasted_iota(jnp.int32, (rows, group), 1)
    live = (column == dp * rows + row) & (row < counts_ref[dp])
    table[mine, width:full] = lax.dot_general(
        jnp.where(live, 1.0, 0.0).astype(jnp.bfloat16), split,
        (((1,), (1,)), ((), ())), preferred_element_type=jnp.float32,
    ).astype(jnp.bfloat16)

    barrier = pltpu.get_barrier_semaphore()
    peers = line + [y_peer, x_peer, core_peer]
    for peer in peers:
        pl.semaphore_signal(barrier, inc=1, device_id=peer, device_id_type=MESH)
    pl.semaphore_wait(barrier, len(peers))

    def remote(source, target, send, recv, peer):
        return pltpu.make_async_remote_copy(
            src_ref=source, dst_ref=target, send_sem=send, recv_sem=recv,
            device_id=peer, device_id_type=MESH,
        )

    def spread(kind, k, start, lo, hi, peer):
        piece = table.at[pl.ds(start, rows), lo:hi]
        return remote(piece, piece, gs.at[kind, k], gr.at[kind, k], peer)

    sent = []

    def send(*what):
        copy = spread(*what)
        copy.start()
        sent.append(copy)

    start_own = place(c, y, x, z)
    own_piece = table.at[pl.ds(start_own, rows), :]
    own_above = remote(own_piece, own_piece, gs.at[0, z], gr.at[0, z], above)
    own_below = remote(own_piece, own_piece, gs.at[9, z], gr.at[0, z], below)
    chain = [(z + 1 < depth, own_above), (z > 0, own_below)]
    pl.when(z + 1 < depth)(own_above.start)
    pl.when(z > 0)(own_below.start)
    for k in range(depth):
        here = place(c, y, x, came[k])
        if k > 0:
            source = came[k]
            spread(0, source, here, 0, full, above).wait_recv()
            rising = source < z
            onward = jnp.where(rising, z + 1, z - 1)
            passes = (onward >= 0) & (onward < depth)
            relay = spread(0, source, here, 0, full, device(onward, y, x, c))
            pl.when(passes)(relay.start)
            chain.append((passes, relay))
        send(1, k, here, 0, full, y_peer)
        send(2, k, here, 0, full, x_peer)
        send(5, k, here, 0, full, core_peer)
    for k in range(depth):
        here = place(c, 1 - y, x, came[k])
        spread(1, k, here, 0, full, y_peer).wait_recv()
        send(3, k, here, 0, half, x_peer)
        send(6, k, here, 0, full, core_peer)
        here = place(c, y, 1 - x, came[k])
        spread(2, k, here, 0, full, x_peer).wait_recv()
        send(4, k, here, half, full, y_peer)
        send(7, k, here, 0, full, core_peer)

    def finish_gather():
        for k in range(depth):
            here = place(c, 1 - y, 1 - x, came[k])
            spread(3, k, here, 0, half, x_peer).wait_recv()
            spread(4, k, here, half, full, y_peer).wait_recv()
            send(8, k, here, 0, full, core_peer)

    def meet(kind, py, px):
        for k in range(depth):
            spread(kind, k, place(1 - c, py, px, came[k]), 0, full, core_peer).wait_recv()

    block = depth * rows
    chunk = 2 * block
    first = ep * local_experts
    tile = 512 if width % 512 == 0 else LANES
    order = list(range(1, depth)) + [0]

    def emit(copy):
        copy.start()
        sent.append(copy)

    def across(i, py):
        piece = pl.ds(place(1 - c, py, 0, 0), chunk)
        landing = pl.ds(pl.multiple_of(py * chunk, chunk), chunk)
        return remote(partial.at[piece], from_core.at[landing], rs.at[0, i], rr.at[0, i], core_peer)

    def slot(py, px, k):
        return pl.ds(place(c, py, px, hops[k]), rows)

    def spot(k):
        return pl.ds(pl.multiple_of(hops[k] * rows, rows), rows)

    def corner(side, k):
        lo, hi = (0, half) if side == 0 else (half, width)
        piece = partial.at[slot(1 - y, 1 - x, k), lo:hi]
        landing = from_diag.at[spot(k), lo:hi]
        peer = x_peer if side == 0 else y_peer
        return remote(piece, landing, rs.at[1 + side, k], rr.at[1 + side, k], peer)

    def side_copy(kind, k):
        py, px, peer, side = (y, 1 - x, x_peer, 1) if kind < 5 else (1 - y, x, y_peer, 0)
        lo, hi = (0, half) if kind in (3, 6) else (half, width)
        piece = partial.at[slot(py, px, k), lo:hi]
        landing = from_side.at[side, spot(k), lo:hi]
        return remote(piece, landing, rs.at[kind, k], rr.at[kind, k], peer)

    def add_core(py, px, k):
        here = slot(py, px, k)
        there = pl.ds(pl.multiple_of(((py * 2 + px) * depth + hops[k]) * rows, rows), rows)
        total = partial[here, :].astype(jnp.float32) + from_core[there, :].astype(jnp.float32)
        partial[here, :] = total.astype(jnp.bfloat16)

    def early():
        across(0, y).wait_recv()
        for k in order:
            add_core(y, 1 - x, k)
            emit(side_copy(3, k))
        for k in order:
            add_core(y, x, k)

    def compute(i, py, between, before_down):
        start = place(0, py, 0, 0)
        span = pl.ds(start, 2 * chunk)
        extra = table[span, width:full].astype(jnp.float32)
        lanes = lax.broadcasted_iota(jnp.int32, (2 * chunk, LANES), 1)
        for j in range(local_experts):
            pick = (lanes == first + j) | (lanes == experts_all + first + j)
            share = jnp.sum(jnp.where(pick, extra, 0.0), axis=1, keepdims=True)
            gate = jnp.dot(table[span, 0:width], gate_mat[j], preferred_element_type=jnp.float32)
            up = jnp.dot(table[span, 0:width], up_mat[j], preferred_element_type=jnp.float32)
            value = gate / (1.0 + jnp.exp(-gate)) * up * share
            hidden_rows[:, j * hidden : (j + 1) * hidden] = value.astype(jnp.bfloat16)
            if j == 0:
                between()
        before_down()
        for core in (1 - c, c):
            both = hidden_rows[pl.ds(pl.multiple_of(core * chunk, chunk), chunk), :]
            target = pl.ds(place(core, py, 0, 0), chunk)

            @pl.loop(0, width // tile)
            def _(n):
                columns = pl.ds(pl.multiple_of(n * tile, tile), tile)
                partial[target, columns] = jnp.dot(
                    both, down_mat[:, columns], preferred_element_type=jnp.float32
                ).astype(jnp.bfloat16)

            if core is not c:
                emit(across(i, py))

    def nothing():
        pass

    for load in loads:
        load.wait()
    meet(5, y, x)
    meet(7, y, 1 - x)
    compute(0, y, nothing, finish_gather)
    meet(6, 1 - y, x)
    meet(8, 1 - y, 1 - x)
    compute(1, 1 - y, early, nothing)

    across(1, 1 - y).wait_recv()
    for k in order:
        add_core(1 - y, 1 - x, k)
        emit(corner(0, k))
        emit(corner(1, k))
    for k in order:
        add_core(1 - y, x, k)
        emit(side_copy(5, k))

    for k in order:
        for side, kind, py, px in ((0, 6, 1 - y, x), (1, 4, y, 1 - x)):
            corner(side, k).wait_recv()
            lo, hi = (0, half) if side == 0 else (half, width)
            here, there = slot(py, px, k), spot(k)
            total = partial[here, lo:hi].astype(jnp.float32) + from_diag[there, lo:hi].astype(jnp.float32)
            partial[here, lo:hi] = total.astype(jnp.bfloat16)
            emit(side_copy(kind, k))

    def line_copy(k):
        piece = partial.at[slot(y, x, k)]
        return remote(piece, from_line.at[k - 1], rs.at[7, k], rr.at[7, k], line[k - 1])

    def settle(k):
        for kind in (3, 4, 5, 6):
            side_copy(kind, k).wait_recv()
        there = spot(k)
        total = partial[slot(y, x, k), :].astype(jnp.float32) + from_side[0, there, :].astype(jnp.float32)
        return total + from_side[1, there, :].astype(jnp.float32)

    for k in range(1, depth):
        partial[slot(y, x, k), :] = settle(k).astype(jnp.bfloat16)
        emit(line_copy(k))
    total = settle(0)
    for k in range(1, depth):
        line_copy(k).wait_recv()
        total += from_line[k - 1].astype(jnp.float32)
    out_ref[...] = total.astype(out_ref.dtype)

    for copy in sent:
        copy.wait_send()
    for done, copy in chain:
        pl.when(done)(copy.wait_send)


def fused_body(tokens, expert_ids, gate_weights, live_counts, w_gate, w_up, w_down):
    depth = lax.axis_size("ep") // 2
    rows, width = tokens.shape
    local_experts, _, hidden = w_gate.shape
    everyone = depth * 8 * rows
    vmem, hbm = pl.BlockSpec(memory_space=pltpu.VMEM), pl.BlockSpec(memory_space=pl.ANY)
    weights = local_experts * width * hidden
    return pl.pallas_call(
        fused_kernel,
        out_shape=jax.ShapeDtypeStruct((rows, width), tokens.dtype),
        in_specs=[vmem, vmem, vmem, pl.BlockSpec(memory_space=pltpu.SMEM), hbm, hbm, hbm],
        out_specs=vmem,
        scratch_shapes=[
            pltpu.VMEM((everyone, width + LANES), jnp.bfloat16),
            pltpu.VMEM((everyone, width), jnp.bfloat16),
            pltpu.VMEM((everyone // 2, width), jnp.bfloat16),
            pltpu.VMEM((depth * rows, width), jnp.bfloat16),
            pltpu.VMEM((2, depth * rows, width), jnp.bfloat16),
            pltpu.VMEM((depth - 1, rows, width), jnp.bfloat16),
            pltpu.VMEM((local_experts, width, hidden), jnp.bfloat16),
            pltpu.VMEM((local_experts, width, hidden), jnp.bfloat16),
            pltpu.VMEM((local_experts * hidden, width), jnp.bfloat16),
            pltpu.VMEM((everyone // 2, local_experts * hidden), jnp.bfloat16),
            pltpu.SemaphoreType.DMA((3 * local_experts,)),
            pltpu.SemaphoreType.DMA((10, depth)),
            pltpu.SemaphoreType.DMA((10, depth)),
            pltpu.SemaphoreType.DMA((8, max(depth, 2))),
            pltpu.SemaphoreType.DMA((8, max(depth, 2))),
        ],
        compiler_params=pltpu.CompilerParams(
            collective_id=0, has_side_effects=True, vmem_limit_bytes=56 << 20
        ),
        cost_estimate=pl.CostEstimate(
            flops=6 * everyone * weights, bytes_accessed=6 * weights, transcendentals=0
        ),
    )(tokens, expert_ids.T, gate_weights.T, live_counts, w_gate, w_up, w_down)


def body(tokens, expert_ids, gate_weights, live_counts, w_gate, w_up, w_down):
    operands = (tokens, expert_ids, gate_weights, live_counts, w_gate, w_up, w_down)
    ep_count, dp_count = lax.axis_size("ep"), lax.axis_size("dp")
    experts_all = w_gate.shape[0] * ep_count
    capacity = 2 * expert_ids.shape[0] * expert_ids.shape[1] // experts_all
    if capacity >= expert_ids.shape[0] and ep_count == 8 and dp_count == 4:
        return fused_body(*operands)
    return slot_body(*operands)


def solution(mesh):
    placed = (
        P(("ep", "dp"), None),
        P("ep", None),
        P("ep", None),
        P("ep"),
        P("ep", None, "dp"),
        P("ep", None, "dp"),
        P("ep", "dp", None),
    )
    return jax.shard_map(
        body, mesh=mesh, in_specs=placed, out_specs=P(("ep", "dp"), None), check_vma=False
    )
```

```python
import jax
import jax.numpy as jnp
from jax import lax
from jax.experimental import pallas as pl
from jax.experimental.pallas import tpu as pltpu
from jax.sharding import PartitionSpec as P


def slot_table(block_ids, block_counts, experts_all, capacity):
    row_count = block_ids.shape[0]
    top_count = block_ids.shape[1]
    per_device = row_count // block_counts.shape[0]
    positions = jnp.arange(row_count, dtype=jnp.int32)
    owners = positions // per_device
    device_ids = jnp.arange(block_counts.shape[0], dtype=jnp.int32)
    limits = jnp.sum(
        jnp.where(owners[:, None] == device_ids[None, :], block_counts[None, :], 0),
        axis=1,
        dtype=jnp.int32,
    )
    live_mask = positions % per_device < limits
    flat_ids = block_ids.reshape(-1)
    live_pairs = jnp.repeat(live_mask, top_count)
    expert_range = jnp.arange(experts_all, dtype=jnp.int32)
    one_hot = jnp.where(
        (flat_ids[:, None] == expert_range[None, :]) & live_pairs[:, None], 1, 0
    ).astype(jnp.int32)
    earlier = jnp.cumsum(one_hot, axis=0, dtype=jnp.int32) - one_hot
    slot_index = jnp.sum(earlier * one_hot, axis=1, dtype=jnp.int32)
    targets = jnp.where(live_pairs, flat_ids * capacity + slot_index, -1)
    return targets.reshape(row_count, top_count)


def expert_apply(slot_rows, gate_mat, up_mat, down_mat):
    gate_part = jnp.einsum(
        "sjnd,jdf->sjnf", slot_rows, gate_mat, preferred_element_type=jnp.float32
    )
    up_part = jnp.einsum("sjnd,jdf->sjnf", slot_rows, up_mat, preferred_element_type=jnp.float32)
    hidden_part = (jax.nn.silu(gate_part) * up_part).astype(jnp.bfloat16)
    return jnp.einsum(
        "sjnf,jfd->sjnd", hidden_part, down_mat, preferred_element_type=jnp.float32
    ).astype(jnp.bfloat16)


def slot_body(tokens, expert_ids, gate_weights, live_counts, w_gate, w_up, w_down):
    ep_count = lax.axis_size("ep")
    local_experts = w_gate.shape[0]
    experts_all = local_experts * ep_count
    block_rows = expert_ids.shape[0]
    top_count = expert_ids.shape[1]
    model_width = tokens.shape[1]
    capacity = 2 * block_rows * top_count // experts_all
    block_tokens = lax.all_gather(tokens, "dp", axis=0, tiled=True)
    targets = slot_table(expert_ids, live_counts, experts_all, capacity)
    slot_range = jnp.arange(experts_all * capacity, dtype=jnp.int32)
    pick_matrix = jnp.sum(
        jnp.where(targets[:, :, None] == slot_range[None, None, :], 1.0, 0.0), axis=1
    ).astype(jnp.bfloat16)
    buffer = jnp.einsum(
        "rs,rd->sd", pick_matrix, block_tokens, preferred_element_type=jnp.float32
    ).astype(jnp.bfloat16)
    buffer = buffer.reshape(ep_count, local_experts, capacity, model_width)
    arrived_rows = lax.all_to_all(buffer, "ep", split_axis=0, concat_axis=0, tiled=True)
    result = expert_apply(arrived_rows, w_gate, w_up, w_down)
    returned = lax.all_to_all(result, "ep", split_axis=0, concat_axis=0, tiled=True)
    live_pairs = targets >= 0
    safe_targets = jnp.maximum(targets, 0)
    table = returned.reshape(experts_all * capacity, model_width)
    picked = jnp.take(table, safe_targets, axis=0).astype(jnp.float32)
    weights = jnp.where(live_pairs, gate_weights, 0.0)
    combined = jnp.sum(weights[:, :, None] * picked, axis=1)
    own_rows = lax.psum_scatter(
        combined.astype(jnp.bfloat16), "dp", scatter_dimension=0, tiled=True
    )
    return own_rows


MESH = pl.DeviceIdType.MESH
LANES = 128


def fused_kernel(
    tokens_ref, ids_ref, gates_ref, counts_ref, gate_hbm, up_hbm, down_hbm, out_ref,
    table, partial, from_core, from_diag, from_side, from_line,
    gate_mat, up_mat, down_mat, hidden_rows, load_sem, gs, gr, rs, rr,
):
    depth = lax.axis_size("ep") // 2
    rows, width = tokens_ref.shape
    local_experts, _, hidden = gate_hbm.shape
    experts_all = local_experts * lax.axis_size("ep")
    ep, dp = lax.axis_index("ep"), lax.axis_index("dp")
    z, y, x, c = ep // 2, ep % 2, dp // 2, dp % 2
    full = width + LANES
    half = (width // LANES // 2) * LANES

    loads = []
    for j in range(local_experts):
        down_rows = down_mat.at[pl.ds(j * hidden, hidden)]
        loads += [(gate_hbm.at[j], gate_mat.at[j]), (up_hbm.at[j], up_mat.at[j]), (down_hbm.at[j], down_rows)]
    loads = [pltpu.make_async_copy(s, d, load_sem.at[i]) for i, (s, d) in enumerate(loads)]
    for load in loads:
        load.start()

    def place(core, py, px, pz):
        return pl.multiple_of((((py * 2 + core) * 2 + px) * depth + pz) * rows, rows)

    def device(pz, py, px, core):
        return (pz * 2 + py, px * 2 + core)

    y_peer, x_peer = device(z, 1 - y, x, c), device(z, y, 1 - x, c)
    core_peer = device(z, y, x, 1 - c)
    hops = [(z + k) % depth for k in range(depth)]
    nearest = [sorted(range(depth), key=lambda o, v=v: (abs(o - v), o)) for v in range(depth)]
    came = [sum(jnp.where(z == v, nearest[v][k], 0) for v in range(depth)) for k in range(depth)]
    above, below = device(z + 1, y, x, c), device(z - 1, y, x, c)
    line = [device(hops[k], y, x, c) for k in range(1, depth)]

    mine = pl.ds(place(c, y, x, z), rows)
    table[mine, 0:width] = tokens_ref[...]
    ids, gates = ids_ref[...], gates_ref[...]
    top, group = ids.shape
    code = lax.broadcasted_iota(jnp.int32, (LANES, group), 0)
    expert = jnp.where(code < experts_all, code, code - experts_all)
    weight = jnp.zeros((LANES, group), jnp.float32)
    for k in range(top):
        weight += jnp.where(ids[k : k + 1, :] == expert, gates[k : k + 1, :], 0.0)
    high = weight.astype(jnp.bfloat16).astype(jnp.float32)
    split = jnp.where(code < experts_all, high, weight - high)
    split = jnp.where(code < 2 * experts_all, split, 0.0).astype(jnp.bfloat16)
    row = lax.broadcasted_iota(jnp.int32, (rows, group), 0)
    column = lax.broadcasted_iota(jnp.int32, (rows, group), 1)
    live = (column == dp * rows + row) & (row < counts_ref[dp])
    table[mine, width:full] = lax.dot_general(
        jnp.where(live, 1.0, 0.0).astype(jnp.bfloat16), split,
        (((1,), (1,)), ((), ())), preferred_element_type=jnp.float32,
    ).astype(jnp.bfloat16)

    barrier = pltpu.get_barrier_semaphore()
    peers = line + [y_peer, x_peer, core_peer]
    for peer in peers:
        pl.semaphore_signal(barrier, inc=1, device_id=peer, device_id_type=MESH)
    pl.semaphore_wait(barrier, len(peers))

    def remote(source, target, send, recv, peer):
        return pltpu.make_async_remote_copy(
            src_ref=source, dst_ref=target, send_sem=send, recv_sem=recv,
            device_id=peer, device_id_type=MESH,
        )

    def spread(kind, k, start, lo, hi, peer):
        piece = table.at[pl.ds(start, rows), lo:hi]
        return remote(piece, piece, gs.at[kind, k], gr.at[kind, k], peer)

    sent = []

    def send(*what):
        copy = spread(*what)
        copy.start()
        sent.append(copy)

    start_own = place(c, y, x, z)
    own_piece = table.at[pl.ds(start_own, rows), :]
    own_above = remote(own_piece, own_piece, gs.at[0, z], gr.at[0, z], above)
    own_below = remote(own_piece, own_piece, gs.at[9, z], gr.at[0, z], below)
    chain = [(z + 1 < depth, own_above), (z > 0, own_below)]
    pl.when(z + 1 < depth)(own_above.start)
    pl.when(z > 0)(own_below.start)
    for k in range(depth):
        here = place(c, y, x, came[k])
        if k > 0:
            source = came[k]
            spread(0, source, here, 0, full, above).wait_recv()
            rising = source < z
            onward = jnp.where(rising, z + 1, z - 1)
            passes = (onward >= 0) & (onward < depth)
            relay = spread(0, source, here, 0, full, device(onward, y, x, c))
            pl.when(passes)(relay.start)
            chain.append((passes, relay))
        send(1, k, here, 0, full, y_peer)
        send(2, k, here, 0, full, x_peer)
        send(5, k, here, 0, full, core_peer)
    for k in range(depth):
        here = place(c, 1 - y, x, came[k])
        spread(1, k, here, 0, full, y_peer).wait_recv()
        send(3, k, here, 0, half, x_peer)
        send(6, k, here, 0, full, core_peer)
        here = place(c, y, 1 - x, came[k])
        spread(2, k, here, 0, full, x_peer).wait_recv()
        send(4, k, here, half, full, y_peer)
        send(7, k, here, 0, full, core_peer)

    def finish_gather():
        for k in range(depth):
            here = place(c, 1 - y, 1 - x, came[k])
            spread(3, k, here, 0, half, x_peer).wait_recv()
            spread(4, k, here, half, full, y_peer).wait_recv()
            send(8, k, here, 0, full, core_peer)

    def meet(kind, py, px):
        for k in range(depth):
            spread(kind, k, place(1 - c, py, px, came[k]), 0, full, core_peer).wait_recv()

    block = depth * rows
    chunk = 2 * block
    first = ep * local_experts
    tile = 512 if width % 512 == 0 else LANES
    order = list(range(1, depth)) + [0]

    def emit(copy):
        copy.start()
        sent.append(copy)

    def across(i, py):
        piece = pl.ds(place(1 - c, py, 0, 0), chunk)
        landing = pl.ds(pl.multiple_of(py * chunk, chunk), chunk)
        return remote(partial.at[piece], from_core.at[landing], rs.at[0, i], rr.at[0, i], core_peer)

    def slot(py, px, k):
        return pl.ds(place(c, py, px, hops[k]), rows)

    def spot(k):
        return pl.ds(pl.multiple_of(hops[k] * rows, rows), rows)

    cut = (width // LANES * 3 // 4) * LANES

    def corner(side, k):
        lo, hi = (0, cut) if side == 0 else (cut, width)
        piece = partial.at[slot(1 - y, 1 - x, k), lo:hi]
        landing = from_diag.at[spot(k), lo:hi]
        peer = x_peer if side == 0 else y_peer
        return remote(piece, landing, rs.at[1 + side, k], rr.at[1 + side, k], peer)

    def side_copy(kind, k):
        py, px, peer, side = (y, 1 - x, x_peer, 1) if kind < 5 else (1 - y, x, y_peer, 0)
        lo, hi = (0, cut) if kind in (3, 6) else (cut, width)
        piece = partial.at[slot(py, px, k), lo:hi]
        landing = from_side.at[side, spot(k), lo:hi]
        return remote(piece, landing, rs.at[kind, k], rr.at[kind, k], peer)

    def add_core(py, px, k):
        here = slot(py, px, k)
        there = pl.ds(pl.multiple_of(((py * 2 + px) * depth + hops[k]) * rows, rows), rows)
        total = partial[here, :].astype(jnp.float32) + from_core[there, :].astype(jnp.float32)
        partial[here, :] = total.astype(jnp.bfloat16)

    def early():
        across(0, y).wait_recv()
        for k in order:
            add_core(y, 1 - x, k)
            emit(side_copy(3, k))
        for k in order:
            add_core(y, x, k)

    def compute(i, py, between, before_down):
        start = place(0, py, 0, 0)
        span = pl.ds(start, 2 * chunk)
        extra = table[span, width:full].astype(jnp.float32)
        lanes = lax.broadcasted_iota(jnp.int32, (2 * chunk, LANES), 1)
        for j in range(local_experts):
            pick = (lanes == first + j) | (lanes == experts_all + first + j)
            share = jnp.sum(jnp.where(pick, extra, 0.0), axis=1, keepdims=True)
            gate = jnp.dot(table[span, 0:width], gate_mat[j], preferred_element_type=jnp.float32)
            up = jnp.dot(table[span, 0:width], up_mat[j], preferred_element_type=jnp.float32)
            value = gate / (1.0 + jnp.exp(-gate)) * up * share
            hidden_rows[:, j * hidden : (j + 1) * hidden] = value.astype(jnp.bfloat16)
            if j == 0:
                between()
        before_down()
        for core in (1 - c, c):
            both = hidden_rows[pl.ds(pl.multiple_of(core * chunk, chunk), chunk), :]
            target = pl.ds(place(core, py, 0, 0), chunk)

            @pl.loop(0, width // tile)
            def _(n):
                columns = pl.ds(pl.multiple_of(n * tile, tile), tile)
                partial[target, columns] = jnp.dot(
                    both, down_mat[:, columns], preferred_element_type=jnp.float32
                ).astype(jnp.bfloat16)

            if core is not c:
                emit(across(i, py))

    def nothing():
        pass

    for load in loads:
        load.wait()
    meet(5, y, x)
    meet(7, y, 1 - x)
    compute(0, y, nothing, finish_gather)
    meet(6, 1 - y, x)
    meet(8, 1 - y, 1 - x)
    compute(1, 1 - y, early, nothing)

    across(1, 1 - y).wait_recv()
    for k in order:
        add_core(1 - y, 1 - x, k)
        emit(corner(0, k))
        emit(corner(1, k))
    for k in order:
        add_core(1 - y, x, k)
        emit(side_copy(5, k))

    for k in order:
        for side, kind, py, px in ((0, 6, 1 - y, x), (1, 4, y, 1 - x)):
            corner(side, k).wait_recv()
            lo, hi = (0, cut) if side == 0 else (cut, width)
            here, there = slot(py, px, k), spot(k)
            total = partial[here, lo:hi].astype(jnp.float32) + from_diag[there, lo:hi].astype(jnp.float32)
            partial[here, lo:hi] = total.astype(jnp.bfloat16)
            emit(side_copy(kind, k))

    def line_copy(k):
        piece = partial.at[slot(y, x, k)]
        return remote(piece, from_line.at[k - 1], rs.at[7, k], rr.at[7, k], line[k - 1])

    def settle(k):
        for kind in (3, 4, 5, 6):
            side_copy(kind, k).wait_recv()
        there = spot(k)
        total = partial[slot(y, x, k), :].astype(jnp.float32) + from_side[0, there, :].astype(jnp.float32)
        return total + from_side[1, there, :].astype(jnp.float32)

    for k in range(1, depth):
        partial[slot(y, x, k), :] = settle(k).astype(jnp.bfloat16)
        emit(line_copy(k))
    total = settle(0)
    for k in range(1, depth):
        line_copy(k).wait_recv()
        total += from_line[k - 1].astype(jnp.float32)
    out_ref[...] = total.astype(out_ref.dtype)

    for copy in sent:
        copy.wait_send()
    for done, copy in chain:
        pl.when(done)(copy.wait_send)


def fused_body(tokens, expert_ids, gate_weights, live_counts, w_gate, w_up, w_down):
    depth = lax.axis_size("ep") // 2
    rows, width = tokens.shape
    local_experts, _, hidden = w_gate.shape
    everyone = depth * 8 * rows
    vmem, hbm = pl.BlockSpec(memory_space=pltpu.VMEM), pl.BlockSpec(memory_space=pl.ANY)
    weights = local_experts * width * hidden
    return pl.pallas_call(
        fused_kernel,
        out_shape=jax.ShapeDtypeStruct((rows, width), tokens.dtype),
        in_specs=[vmem, vmem, vmem, pl.BlockSpec(memory_space=pltpu.SMEM), hbm, hbm, hbm],
        out_specs=vmem,
        scratch_shapes=[
            pltpu.VMEM((everyone, width + LANES), jnp.bfloat16),
            pltpu.VMEM((everyone, width), jnp.bfloat16),
            pltpu.VMEM((everyone // 2, width), jnp.bfloat16),
            pltpu.VMEM((depth * rows, width), jnp.bfloat16),
            pltpu.VMEM((2, depth * rows, width), jnp.bfloat16),
            pltpu.VMEM((depth - 1, rows, width), jnp.bfloat16),
            pltpu.VMEM((local_experts, width, hidden), jnp.bfloat16),
            pltpu.VMEM((local_experts, width, hidden), jnp.bfloat16),
            pltpu.VMEM((local_experts * hidden, width), jnp.bfloat16),
            pltpu.VMEM((everyone // 2, local_experts * hidden), jnp.bfloat16),
            pltpu.SemaphoreType.DMA((3 * local_experts,)),
            pltpu.SemaphoreType.DMA((10, depth)),
            pltpu.SemaphoreType.DMA((10, depth)),
            pltpu.SemaphoreType.DMA((8, max(depth, 2))),
            pltpu.SemaphoreType.DMA((8, max(depth, 2))),
        ],
        compiler_params=pltpu.CompilerParams(
            collective_id=0, has_side_effects=True, vmem_limit_bytes=56 << 20
        ),
        cost_estimate=pl.CostEstimate(
            flops=6 * everyone * weights, bytes_accessed=6 * weights, transcendentals=0
        ),
    )(tokens, expert_ids.T, gate_weights.T, live_counts, w_gate, w_up, w_down)


def body(tokens, expert_ids, gate_weights, live_counts, w_gate, w_up, w_down):
    operands = (tokens, expert_ids, gate_weights, live_counts, w_gate, w_up, w_down)
    ep_count, dp_count = lax.axis_size("ep"), lax.axis_size("dp")
    experts_all = w_gate.shape[0] * ep_count
    capacity = 2 * expert_ids.shape[0] * expert_ids.shape[1] // experts_all
    if capacity >= expert_ids.shape[0] and ep_count == 8 and dp_count == 4:
        return fused_body(*operands)
    return slot_body(*operands)


def solution(mesh):
    placed = (
        P(("ep", "dp"), None),
        P("ep", None),
        P("ep", None),
        P("ep"),
        P("ep", None, "dp"),
        P("ep", None, "dp"),
        P("ep", "dp", None),
    )
    return jax.shard_map(
        body, mesh=mesh, in_specs=placed, out_specs=P(("ep", "dp"), None), check_vma=False
    )
```

```python
import jax
import jax.numpy as jnp
from jax import lax
from jax.experimental import pallas as pl
from jax.experimental.pallas import tpu as pltpu
from jax.sharding import PartitionSpec as P


def slot_table(block_ids, block_counts, experts_all, capacity):
    row_count = block_ids.shape[0]
    top_count = block_ids.shape[1]
    per_device = row_count // block_counts.shape[0]
    positions = jnp.arange(row_count, dtype=jnp.int32)
    owners = positions // per_device
    device_ids = jnp.arange(block_counts.shape[0], dtype=jnp.int32)
    limits = jnp.sum(
        jnp.where(owners[:, None] == device_ids[None, :], block_counts[None, :], 0),
        axis=1,
        dtype=jnp.int32,
    )
    live_mask = positions % per_device < limits
    flat_ids = block_ids.reshape(-1)
    live_pairs = jnp.repeat(live_mask, top_count)
    expert_range = jnp.arange(experts_all, dtype=jnp.int32)
    one_hot = jnp.where(
        (flat_ids[:, None] == expert_range[None, :]) & live_pairs[:, None], 1, 0
    ).astype(jnp.int32)
    earlier = jnp.cumsum(one_hot, axis=0, dtype=jnp.int32) - one_hot
    slot_index = jnp.sum(earlier * one_hot, axis=1, dtype=jnp.int32)
    targets = jnp.where(live_pairs, flat_ids * capacity + slot_index, -1)
    return targets.reshape(row_count, top_count)


def expert_apply(slot_rows, gate_mat, up_mat, down_mat):
    gate_part = jnp.einsum(
        "sjnd,jdf->sjnf", slot_rows, gate_mat, preferred_element_type=jnp.float32
    )
    up_part = jnp.einsum("sjnd,jdf->sjnf", slot_rows, up_mat, preferred_element_type=jnp.float32)
    hidden_part = (jax.nn.silu(gate_part) * up_part).astype(jnp.bfloat16)
    return jnp.einsum(
        "sjnf,jfd->sjnd", hidden_part, down_mat, preferred_element_type=jnp.float32
    ).astype(jnp.bfloat16)


def slot_body(tokens, expert_ids, gate_weights, live_counts, w_gate, w_up, w_down):
    ep_count = lax.axis_size("ep")
    local_experts = w_gate.shape[0]
    experts_all = local_experts * ep_count
    block_rows = expert_ids.shape[0]
    top_count = expert_ids.shape[1]
    model_width = tokens.shape[1]
    capacity = 2 * block_rows * top_count // experts_all
    block_tokens = lax.all_gather(tokens, "dp", axis=0, tiled=True)
    targets = slot_table(expert_ids, live_counts, experts_all, capacity)
    slot_range = jnp.arange(experts_all * capacity, dtype=jnp.int32)
    pick_matrix = jnp.sum(
        jnp.where(targets[:, :, None] == slot_range[None, None, :], 1.0, 0.0), axis=1
    ).astype(jnp.bfloat16)
    buffer = jnp.einsum(
        "rs,rd->sd", pick_matrix, block_tokens, preferred_element_type=jnp.float32
    ).astype(jnp.bfloat16)
    buffer = buffer.reshape(ep_count, local_experts, capacity, model_width)
    arrived_rows = lax.all_to_all(buffer, "ep", split_axis=0, concat_axis=0, tiled=True)
    result = expert_apply(arrived_rows, w_gate, w_up, w_down)
    returned = lax.all_to_all(result, "ep", split_axis=0, concat_axis=0, tiled=True)
    live_pairs = targets >= 0
    safe_targets = jnp.maximum(targets, 0)
    table = returned.reshape(experts_all * capacity, model_width)
    picked = jnp.take(table, safe_targets, axis=0).astype(jnp.float32)
    weights = jnp.where(live_pairs, gate_weights, 0.0)
    combined = jnp.sum(weights[:, :, None] * picked, axis=1)
    own_rows = lax.psum_scatter(
        combined.astype(jnp.bfloat16), "dp", scatter_dimension=0, tiled=True
    )
    return own_rows


MESH = pl.DeviceIdType.MESH
LANES = 128


def fused_kernel(
    tokens_ref, ids_ref, gates_ref, counts_ref, gate_hbm, up_hbm, down_hbm, out_ref,
    table, partial, from_core, from_diag, from_side, from_line,
    gate_mat, up_mat, down_mat, hidden_rows, load_sem, gs, gr, rs, rr,
):
    depth = lax.axis_size("ep") // 2
    rows, width = tokens_ref.shape
    local_experts, _, hidden = gate_hbm.shape
    experts_all = local_experts * lax.axis_size("ep")
    ep, dp = lax.axis_index("ep"), lax.axis_index("dp")
    z, y, x, c = ep // 2, ep % 2, dp // 2, dp % 2
    full = width + LANES
    half = (width // LANES // 2) * LANES

    loads = []
    for j in range(local_experts):
        down_rows = down_mat.at[pl.ds(j * hidden, hidden)]
        loads += [(gate_hbm.at[j], gate_mat.at[j]), (up_hbm.at[j], up_mat.at[j]), (down_hbm.at[j], down_rows)]
    loads = [pltpu.make_async_copy(s, d, load_sem.at[i]) for i, (s, d) in enumerate(loads)]
    for load in loads:
        load.start()

    def place(core, py, px, pz):
        return pl.multiple_of((((py * 2 + core) * 2 + px) * depth + pz) * rows, rows)

    def device(pz, py, px, core):
        return (pz * 2 + py, px * 2 + core)

    y_peer, x_peer = device(z, 1 - y, x, c), device(z, y, 1 - x, c)
    core_peer = device(z, y, x, 1 - c)
    hops = [(z + k) % depth for k in range(depth)]
    nearest = [sorted(range(depth), key=lambda o, v=v: (abs(o - v), o)) for v in range(depth)]
    came = [sum(jnp.where(z == v, nearest[v][k], 0) for v in range(depth)) for k in range(depth)]
    above, below = device(z + 1, y, x, c), device(z - 1, y, x, c)
    line = [device(hops[k], y, x, c) for k in range(1, depth)]

    mine = pl.ds(place(c, y, x, z), rows)
    table[mine, 0:width] = tokens_ref[...]
    ids, gates = ids_ref[...], gates_ref[...]
    top, group = ids.shape
    code = lax.broadcasted_iota(jnp.int32, (LANES, group), 0)
    expert = jnp.where(code < experts_all, code, code - experts_all)
    weight = jnp.zeros((LANES, group), jnp.float32)
    for k in range(top):
        weight += jnp.where(ids[k : k + 1, :] == expert, gates[k : k + 1, :], 0.0)
    high = weight.astype(jnp.bfloat16).astype(jnp.float32)
    split = jnp.where(code < experts_all, high, weight - high)
    split = jnp.where(code < 2 * experts_all, split, 0.0).astype(jnp.bfloat16)
    row = lax.broadcasted_iota(jnp.int32, (rows, group), 0)
    column = lax.broadcasted_iota(jnp.int32, (rows, group), 1)
    live = (column == dp * rows + row) & (row < counts_ref[dp])
    table[mine, width:full] = lax.dot_general(
        jnp.where(live, 1.0, 0.0).astype(jnp.bfloat16), split,
        (((1,), (1,)), ((), ())), preferred_element_type=jnp.float32,
    ).astype(jnp.bfloat16)

    barrier = pltpu.get_barrier_semaphore()
    peers = line + [y_peer, x_peer, core_peer]
    for peer in peers:
        pl.semaphore_signal(barrier, inc=1, device_id=peer, device_id_type=MESH)
    pl.semaphore_wait(barrier, len(peers))

    def remote(source, target, send, recv, peer):
        return pltpu.make_async_remote_copy(
            src_ref=source, dst_ref=target, send_sem=send, recv_sem=recv,
            device_id=peer, device_id_type=MESH,
        )

    def spread(kind, k, start, lo, hi, peer):
        piece = table.at[pl.ds(start, rows), lo:hi]
        return remote(piece, piece, gs.at[kind, k], gr.at[kind, k], peer)

    sent = []

    def send(*what):
        copy = spread(*what)
        copy.start()
        sent.append(copy)

    start_own = place(c, y, x, z)
    own_piece = table.at[pl.ds(start_own, rows), :]
    own_above = remote(own_piece, own_piece, gs.at[0, z], gr.at[0, z], above)
    own_below = remote(own_piece, own_piece, gs.at[9, z], gr.at[0, z], below)
    chain = [(z + 1 < depth, own_above), (z > 0, own_below)]
    pl.when(z + 1 < depth)(own_above.start)
    pl.when(z > 0)(own_below.start)
    for k in range(depth):
        here = place(c, y, x, came[k])
        if k > 0:
            source = came[k]
            spread(0, source, here, 0, full, above).wait_recv()
            rising = source < z
            onward = jnp.where(rising, z + 1, z - 1)
            passes = (onward >= 0) & (onward < depth)
            relay = spread(0, source, here, 0, full, device(onward, y, x, c))
            pl.when(passes)(relay.start)
            chain.append((passes, relay))
        send(2, k, here, 0, full, x_peer)
        send(1, k, here, 0, full, y_peer)
        if k > 0:
            send(5, k - 1, place(c, y, x, came[k - 1]), 0, full, core_peer)
    send(5, depth - 1, place(c, y, x, came[depth - 1]), 0, full, core_peer)
    for k in range(depth):
        here = place(c, 1 - y, x, came[k])
        spread(1, k, here, 0, full, y_peer).wait_recv()
        send(3, k, here, 0, half, x_peer)
        send(6, k, here, 0, full, core_peer)
        here = place(c, y, 1 - x, came[k])
        spread(2, k, here, 0, full, x_peer).wait_recv()
        send(4, k, here, half, full, y_peer)
        send(7, k, here, 0, full, core_peer)

    def finish_gather():
        for k in range(depth):
            here = place(c, 1 - y, 1 - x, came[k])
            spread(3, k, here, 0, half, x_peer).wait_recv()
            spread(4, k, here, half, full, y_peer).wait_recv()
            send(8, k, here, 0, full, core_peer)

    def meet(kind, py, px):
        for k in range(depth):
            spread(kind, k, place(1 - c, py, px, came[k]), 0, full, core_peer).wait_recv()

    block = depth * rows
    chunk = 2 * block
    first = ep * local_experts
    tile = 512 if width % 512 == 0 else LANES
    order = list(range(1, depth)) + [0]

    def emit(copy):
        copy.start()
        sent.append(copy)

    def across(i, py):
        piece = pl.ds(place(1 - c, py, 0, 0), chunk)
        landing = pl.ds(pl.multiple_of(py * chunk, chunk), chunk)
        return remote(partial.at[piece], from_core.at[landing], rs.at[0, i], rr.at[0, i], core_peer)

    def slot(py, px, k):
        return pl.ds(place(c, py, px, hops[k]), rows)

    def spot(k):
        return pl.ds(pl.multiple_of(hops[k] * rows, rows), rows)

    cut = (width // LANES * 3 // 4) * LANES

    def corner(side, k):
        lo, hi = (0, cut) if side == 0 else (cut, width)
        piece = partial.at[slot(1 - y, 1 - x, k), lo:hi]
        landing = from_diag.at[spot(k), lo:hi]
        peer = x_peer if side == 0 else y_peer
        return remote(piece, landing, rs.at[1 + side, k], rr.at[1 + side, k], peer)

    def side_copy(kind, k):
        py, px, peer, side = (y, 1 - x, x_peer, 1) if kind < 5 else (1 - y, x, y_peer, 0)
        lo, hi = (0, cut) if kind in (3, 6) else (cut, width)
        piece = partial.at[slot(py, px, k), lo:hi]
        landing = from_side.at[side, spot(k), lo:hi]
        return remote(piece, landing, rs.at[kind, k], rr.at[kind, k], peer)

    def add_core(py, px, k):
        here = slot(py, px, k)
        there = pl.ds(pl.multiple_of(((py * 2 + px) * depth + hops[k]) * rows, rows), rows)
        total = partial[here, :].astype(jnp.float32) + from_core[there, :].astype(jnp.float32)
        partial[here, :] = total.astype(jnp.bfloat16)

    def early():
        across(0, y).wait_recv()
        for k in order:
            add_core(y, 1 - x, k)
            emit(side_copy(3, k))
        for k in order:
            add_core(y, x, k)

    def compute(i, py, between, before_down, after_send=lambda: None):
        start = place(0, py, 0, 0)
        span = pl.ds(start, 2 * chunk)
        extra = table[span, width:full].astype(jnp.float32)
        lanes = lax.broadcasted_iota(jnp.int32, (2 * chunk, LANES), 1)
        for j in range(local_experts):
            pick = (lanes == first + j) | (lanes == experts_all + first + j)
            share = jnp.sum(jnp.where(pick, extra, 0.0), axis=1, keepdims=True)
            gate = jnp.dot(table[span, 0:width], gate_mat[j], preferred_element_type=jnp.float32)
            up = jnp.dot(table[span, 0:width], up_mat[j], preferred_element_type=jnp.float32)
            value = gate / (1.0 + jnp.exp(-gate)) * up * share
            hidden_rows[:, j * hidden : (j + 1) * hidden] = value.astype(jnp.bfloat16)
            if j == 0:
                between()
        before_down()
        for core in (1 - c, c):
            both = hidden_rows[pl.ds(pl.multiple_of(core * chunk, chunk), chunk), :]
            target = pl.ds(place(core, py, 0, 0), chunk)

            @pl.loop(0, width // tile)
            def _(n):
                columns = pl.ds(pl.multiple_of(n * tile, tile), tile)
                partial[target, columns] = jnp.dot(
                    both, down_mat[:, columns], preferred_element_type=jnp.float32
                ).astype(jnp.bfloat16)

            if core is not c:
                emit(across(i, py))
                after_send()

    def nothing():
        pass

    for load in loads:
        load.wait()
    meet(5, y, x)
    meet(7, y, 1 - x)
    compute(0, y, nothing, nothing, finish_gather)
    meet(6, 1 - y, x)
    meet(8, 1 - y, 1 - x)
    compute(1, 1 - y, early, nothing)

    across(1, 1 - y).wait_recv()
    for k in order:
        add_core(1 - y, 1 - x, k)
        emit(corner(0, k))
        emit(corner(1, k))
    for k in order:
        add_core(1 - y, x, k)
        emit(side_copy(5, k))

    for k in order:
        for side, kind, py, px in ((0, 6, 1 - y, x), (1, 4, y, 1 - x)):
            corner(side, k).wait_recv()
            lo, hi = (0, cut) if side == 0 else (cut, width)
            here, there = slot(py, px, k), spot(k)
            total = partial[here, lo:hi].astype(jnp.float32) + from_diag[there, lo:hi].astype(jnp.float32)
            partial[here, lo:hi] = total.astype(jnp.bfloat16)
            emit(side_copy(kind, k))

    def line_copy(k):
        piece = partial.at[slot(y, x, k)]
        return remote(piece, from_line.at[k - 1], rs.at[7, k], rr.at[7, k], line[k - 1])

    def settle(k):
        for kind in (3, 4, 5, 6):
            side_copy(kind, k).wait_recv()
        there = spot(k)
        total = partial[slot(y, x, k), :].astype(jnp.float32) + from_side[0, there, :].astype(jnp.float32)
        return total + from_side[1, there, :].astype(jnp.float32)

    for k in range(1, depth):
        partial[slot(y, x, k), :] = settle(k).astype(jnp.bfloat16)
        emit(line_copy(k))
    total = settle(0)
    for k in range(1, depth):
        line_copy(k).wait_recv()
        total += from_line[k - 1].astype(jnp.float32)
    out_ref[...] = total.astype(out_ref.dtype)

    for copy in sent:
        copy.wait_send()
    for done, copy in chain:
        pl.when(done)(copy.wait_send)


def fused_body(tokens, expert_ids, gate_weights, live_counts, w_gate, w_up, w_down):
    depth = lax.axis_size("ep") // 2
    rows, width = tokens.shape
    local_experts, _, hidden = w_gate.shape
    everyone = depth * 8 * rows
    vmem, hbm = pl.BlockSpec(memory_space=pltpu.VMEM), pl.BlockSpec(memory_space=pl.ANY)
    weights = local_experts * width * hidden
    return pl.pallas_call(
        fused_kernel,
        out_shape=jax.ShapeDtypeStruct((rows, width), tokens.dtype),
        in_specs=[vmem, vmem, vmem, pl.BlockSpec(memory_space=pltpu.SMEM), hbm, hbm, hbm],
        out_specs=vmem,
        scratch_shapes=[
            pltpu.VMEM((everyone, width + LANES), jnp.bfloat16),
            pltpu.VMEM((everyone, width), jnp.bfloat16),
            pltpu.VMEM((everyone // 2, width), jnp.bfloat16),
            pltpu.VMEM((depth * rows, width), jnp.bfloat16),
            pltpu.VMEM((2, depth * rows, width), jnp.bfloat16),
            pltpu.VMEM((depth - 1, rows, width), jnp.bfloat16),
            pltpu.VMEM((local_experts, width, hidden), jnp.bfloat16),
            pltpu.VMEM((local_experts, width, hidden), jnp.bfloat16),
            pltpu.VMEM((local_experts * hidden, width), jnp.bfloat16),
            pltpu.VMEM((everyone // 2, local_experts * hidden), jnp.bfloat16),
            pltpu.SemaphoreType.DMA((3 * local_experts,)),
            pltpu.SemaphoreType.DMA((10, depth)),
            pltpu.SemaphoreType.DMA((10, depth)),
            pltpu.SemaphoreType.DMA((8, max(depth, 2))),
            pltpu.SemaphoreType.DMA((8, max(depth, 2))),
        ],
        compiler_params=pltpu.CompilerParams(
            collective_id=0, has_side_effects=True, vmem_limit_bytes=56 << 20
        ),
        cost_estimate=pl.CostEstimate(
            flops=6 * everyone * weights, bytes_accessed=6 * weights, transcendentals=0
        ),
    )(tokens, expert_ids.T, gate_weights.T, live_counts, w_gate, w_up, w_down)


def body(tokens, expert_ids, gate_weights, live_counts, w_gate, w_up, w_down):
    operands = (tokens, expert_ids, gate_weights, live_counts, w_gate, w_up, w_down)
    ep_count, dp_count = lax.axis_size("ep"), lax.axis_size("dp")
    experts_all = w_gate.shape[0] * ep_count
    capacity = 2 * expert_ids.shape[0] * expert_ids.shape[1] // experts_all
    if capacity >= expert_ids.shape[0] and ep_count == 8 and dp_count == 4:
        return fused_body(*operands)
    return slot_body(*operands)


def solution(mesh):
    placed = (
        P(("ep", "dp"), None),
        P("ep", None),
        P("ep", None),
        P("ep"),
        P("ep", None, "dp"),
        P("ep", None, "dp"),
        P("ep", "dp", None),
    )
    return jax.shard_map(
        body, mesh=mesh, in_specs=placed, out_specs=P(("ep", "dp"), None), check_vma=False
    )
```
